32 devices in a mesh: rep: 4 (over y, x), shard: 4 (over z), seq: 2 (over core).
Axes of the slice: x: 2, y: 2, z: 4, core: 2. Of those that a mesh axis runs over, the one named last changes fastest.
Arguments:
- tokens: bfloat16 [16, 256, 1024], P(('rep', 'shard'), 'seq'), may hold values from -40 to 40
- key_valid: int32 [16, 256], P(('rep', 'shard')), may hold values from 0 to 1, as said below
- cotangent: bfloat16 [16, 256, 1024], P(('rep', 'shard'), 'seq'), may hold values from -6 to 6
- attngain: bfloat16 [1024], P(('shard', 'seq')), may hold values from 0.5 to 1.5
- attnshift: bfloat16 [1024], P(('shard', 'seq')), may hold values from -4 to 4
- qkvweight: bfloat16 [1024, 3072], P(('shard', 'seq')), may hold values from -3 to 3
- querybias: bfloat16 [1024], P(('shard', 'seq')), may hold values from -4 to 4
- valuebias: bfloat16 [1024], P(('shard', 'seq')), may hold values from -4 to 4
- projweight: bfloat16 [1024, 1024], P(('shard', 'seq')), may hold values from -4 to 4
- projbias: bfloat16 [1024], P(('shard', 'seq')), may hold values from -4 to 4
- attnscale: bfloat16 [1024], P(('shard', 'seq')), may hold values from 0.5 to 1.5
- mlpgain: bfloat16 [1024], P(('shard', 'seq')), may hold values from 0.5 to 1.5
- mlpshift: bfloat16 [1024], P(('shard', 'seq')), may hold values from -4 to 4
- upweight: bfloat16 [1024, 4096], P(('shard', 'seq')), may hold values from -0.1875 to 0.1875
- upbias: bfloat16 [4096], P(('shard', 'seq')), may hold values from -4 to 4
- downweight: bfloat16 [4096, 1024], P(('shard', 'seq')), may hold values from -0.09375 to 0.09375
- downbias: bfloat16 [1024], P(('shard', 'seq')), may hold values from -4 to 4
- mlpscale: bfloat16 [1024], P(('shard', 'seq')), may hold values from 0.5 to 1.5
Outputs:
- block_out: float32 [16, 256, 1024], P(('rep', 'shard'), 'seq')
- grad_tokens: float32 [16, 256, 1024], P(('rep', 'shard'), 'seq')
- grad_attngain: float32 [1024], P(('shard', 'seq'))
- grad_attnshift: float32 [1024], P(('shard', 'seq'))
- grad_qkvweight: float32 [1024, 3072], P(('shard', 'seq'))
- grad_querybias: float32 [1024], P(('shard', 'seq'))
- grad_valuebias: float32 [1024], P(('shard', 'seq'))
- grad_projweight: float32 [1024, 1024], P(('shard', 'seq'))
- grad_projbias: float32 [1024], P(('shard', 'seq'))
- grad_attnscale: float32 [1024], P(('shard', 'seq'))
- grad_mlpgain: float32 [1024], P(('shard', 'seq'))
- grad_mlpshift: float32 [1024], P(('shard', 'seq'))
- grad_upweight: float32 [1024, 4096], P(('shard', 'seq'))
- grad_upbias: float32 [4096], P(('shard', 'seq'))
- grad_downweight: float32 [4096, 1024], P(('shard', 'seq'))
- grad_downbias: float32 [1024], P(('shard', 'seq'))
- grad_mlpscale: float32 [1024], P(('shard', 'seq'))
The draws below stay inside these ranges and needn't reach their ends.
Inputs may be any that keep to these rules, and one draw needn't show every extreme that they name: `key_valid`: in each image the valid positions are its first ones, from 128 to 256 of them; some image has exactly 128, another all 256.
All inputs are finite; a program needn't handle non-finite values.
Results may differ from the reference program's by a relative error of at most 0.011.
Values may be sent and summed in bfloat16 or wider, within the bound.
A program may use at most 192 MiB of HBM per device.

```python
import jax
import jax.numpy as jnp
from jax import lax

D = 1024
FF = 4096
HEADS = 16
HEAD = 64
TOK_DEV = 128
LEN = 256
IMAGES = 16


def draw_tokens(key, part):
    key_one, key_two, key_three = jax.random.split(key, 3)
    normal_part = jax.random.truncated_normal(key_one, -4.0, 4.0, (IMAGES, LEN, D), jnp.float32)
    rowscale = jnp.exp(jax.random.uniform(key_two, (IMAGES, LEN, 1), jnp.float32, -1.2, 1.1))
    colscale = jnp.exp(jax.random.uniform(key_three, (1, 1, D), jnp.float32, -1.2, 1.1))
    values = normal_part * rowscale * colscale
    return values.astype(jnp.bfloat16)


def draw_key_valid(key, part):
    key_one, key_two = jax.random.split(key)
    lengths = jax.random.randint(key_one, (IMAGES,), LEN - TOK_DEV, LEN + 1)
    chosen = jax.random.randint(key_two, (), 0, IMAGES)
    ordinal = jnp.arange(IMAGES)
    lengths = jnp.where(ordinal == chosen, LEN - TOK_DEV, lengths)
    lengths = jnp.where(ordinal == (chosen + 1) % IMAGES, LEN, lengths)
    positions = jnp.arange(LEN)
    return (positions[None, :] < lengths[:, None]).astype(jnp.int32)


def draw_qkvweight(key, part):
    weights = jax.random.truncated_normal(key, -4.0, 4.0, (D, 3 * D), jnp.float32) * D ** (-0.5)
    return weights.astype(jnp.bfloat16)


def level_of(stream_key, shape, cuts, smallest, largest):
    factor_of = 1.0
    for axis_at, blocks in cuts:
        draws = jax.random.uniform(jax.random.fold_in(jax.random.fold_in(stream_key, 6), axis_at), (blocks,), jnp.float32, smallest / len(cuts), largest / len(cuts))
        factor_of = factor_of * jnp.repeat(jnp.exp(draws), shape[axis_at] // blocks).reshape((-1,) + (1,) * (len(shape) - 1 - axis_at))
    return factor_of


def gaussian(own_key, dims, deviation, limit, cuts=(), dtype=jnp.bfloat16):
    array = deviation * jax.random.normal(own_key, dims, jnp.float32)
    if cuts:
        array = array * level_of(own_key, dims, cuts, -0.22, 0.18)
    return jnp.clip(array, -limit, limit).astype(dtype)


def setup_inputs(seed: int = 0) -> dict:
    key_list = jax.random.split(jax.random.key(seed), 19)
    tokens = draw_tokens(jax.random.fold_in(key_list[18], 71), 0)
    key_valid = draw_key_valid(jax.random.fold_in(key_list[18], 71), 0)
    cotangent = gaussian(key_list[2], (IMAGES, LEN, D), 1.0, 6.0, ((0, 16), (1, 2)))
    attngain = jnp.clip(1.0 + 0.1 * jax.random.normal(key_list[3], (D,), jnp.float32), 0.5, 1.5).astype(jnp.bfloat16)
    attnshift = gaussian(key_list[4], (D,), 0.3, 4.0, ((0, 8),))
    qkvweight = draw_qkvweight(jax.random.fold_in(key_list[18], 71), 0)
    querybias = gaussian(key_list[6], (D,), 0.3, 4.0, ((0, 8),))
    valuebias = gaussian(key_list[7], (D,), 0.3, 4.0, ((0, 8),))
    projweight = gaussian(key_list[8], (D, D), 0.7, 4.0, ((0, 8),))
    projbias = gaussian(key_list[9], (D,), 0.3, 4.0, ((0, 8),))
    attnscale = jnp.clip(1.0 + 0.1 * jax.random.normal(key_list[10], (D,), jnp.float32), 0.5, 1.5).astype(jnp.bfloat16)
    mlpgain = jnp.clip(1.0 + 0.1 * jax.random.normal(key_list[11], (D,), jnp.float32), 0.5, 1.5).astype(jnp.bfloat16)
    mlpshift = gaussian(key_list[12], (D,), 0.3, 4.0, ((0, 8),))
    upweight = gaussian(key_list[13], (D, FF), D ** -0.5, 0.1875, ((0, 8),))
    upbias = gaussian(key_list[14], (FF,), 0.5, 4.0, ((0, 8),))
    downweight = gaussian(key_list[15], (FF, D), FF ** -0.5, 0.09375, ((0, 8),))
    downbias = gaussian(key_list[16], (D,), 0.3, 4.0, ((0, 8),))
    mlpscale = jnp.clip(1.0 + 0.1 * jax.random.normal(key_list[17], (D,), jnp.float32), 0.5, 1.5).astype(jnp.bfloat16)
    return dict(tokens=tokens, key_valid=key_valid, cotangent=cotangent, attngain=attngain, attnshift=attnshift, qkvweight=qkvweight, querybias=querybias, valuebias=valuebias, projweight=projweight, projbias=projbias, attnscale=attnscale, mlpgain=mlpgain, mlpshift=mlpshift, upweight=upweight, upbias=upbias, downweight=downweight, downbias=downbias, mlpscale=mlpscale)


EPSILON = 1e-06
SCORE_SCALE = 0.125
ROOT_HALF = 0.7071067811865476
INV_ROOT_TAU = 0.3989422804014327
MASKED = -1e+30

def norm_forward(hidden):
    center = hidden - lax.optimization_barrier(jnp.mean(hidden, axis=-1, keepdims=True))
    spread = lax.rsqrt(lax.optimization_barrier(jnp.mean(center * center, axis=-1, keepdims=True)) + EPSILON)
    return (center * spread, spread)

def norm_backward(grad_norm, normed, spread):
    first_mean = lax.optimization_barrier(jnp.mean(grad_norm, axis=-1, keepdims=True))
    second_mean = lax.optimization_barrier(jnp.mean(grad_norm * normed, axis=-1, keepdims=True))
    return spread * (grad_norm - first_mean - normed * second_mean)

def gelu_pair(hidden):
    cumulative = 0.5 * (1.0 + lax.erf(hidden * ROOT_HALF))
    gelu_slope = cumulative + hidden * jnp.exp(-0.5 * hidden * hidden) * INV_ROOT_TAU
    return (hidden * cumulative, gelu_slope)

def split_heads(matrix):
    return matrix.reshape(LEN, HEADS, HEAD).astype(jnp.float32)

def reference(tokens, key_valid, cotangent, attngain, attnshift, qkvweight, querybias, valuebias, projweight, projbias, attnscale, mlpgain, mlpshift, upweight, upbias, downweight, downbias, mlpscale):
    gain_one = attngain.astype(jnp.float32)
    shift_one = attnshift.astype(jnp.float32)
    qbias_full = querybias.astype(jnp.float32)
    vbias_full = valuebias.astype(jnp.float32)
    pbias_full = projbias.astype(jnp.float32)
    scale_one = attnscale.astype(jnp.float32)
    gain_two = mlpgain.astype(jnp.float32)
    shift_two = mlpshift.astype(jnp.float32)
    upb_full = upbias.astype(jnp.float32)
    downb_full = downbias.astype(jnp.float32)
    scale_two = mlpscale.astype(jnp.float32)

    def image_step(totals, sample):
        image_tokens, image_valid, image_cot = sample
        hidden = image_tokens.astype(jnp.float32)
        normed_one, spread_one = norm_forward(hidden)
        act_one = (normed_one * gain_one + shift_one).astype(jnp.bfloat16)
        mixed = jnp.dot(act_one, qkvweight, preferred_element_type=jnp.float32)
        queries = (mixed[:, :D] + qbias_full).astype(jnp.bfloat16)
        keys_all = mixed[:, D:2 * D].astype(jnp.bfloat16)
        values_all = (mixed[:, 2 * D:] + vbias_full).astype(jnp.bfloat16)
        query_heads = split_heads(queries)
        key_heads = split_heads(keys_all)
        value_heads = split_heads(values_all)
        scores = jnp.einsum('qhe,khe->hqk', query_heads, key_heads) * SCORE_SCALE
        scores = jnp.where((image_valid > 0)[None, None, :], scores, MASKED)
        top_score = lax.optimization_barrier(jnp.max(scores, axis=-1, keepdims=True))
        log_total = top_score + jnp.log(lax.optimization_barrier(jnp.sum(jnp.exp(scores - top_score), axis=-1, keepdims=True)))
        probs = jnp.exp(scores - log_total)
        prob_low = probs.astype(jnp.bfloat16)
        attended = jnp.einsum('hqk,khe->qhe', prob_low.astype(jnp.float32), value_heads).reshape(LEN, D).astype(jnp.bfloat16)
        branch_one = jnp.dot(attended, projweight, preferred_element_type=jnp.float32) + pbias_full
        middle = hidden + scale_one * branch_one
        normed_two, spread_two = norm_forward(middle)
        act_two = (normed_two * gain_two + shift_two).astype(jnp.bfloat16)
        inner_pre = jnp.dot(act_two, upweight, preferred_element_type=jnp.float32) + upb_full
        activated, gelu_slope = gelu_pair(inner_pre)
        act_three = activated.astype(jnp.bfloat16)
        branch_two = jnp.dot(act_three, downweight, preferred_element_type=jnp.float32) + downb_full
        block_out = middle + scale_two * branch_two
        out_grad = image_cot.astype(jnp.float32)
        mlpscale_grad = lax.optimization_barrier(jnp.sum(out_grad * branch_two, axis=0))
        branch_grad = out_grad * scale_two
        downbias_grad = lax.optimization_barrier(jnp.sum(branch_grad, axis=0))
        branch_low = branch_grad.astype(jnp.bfloat16)
        downweight_grad = jnp.dot(act_three.T, branch_low, preferred_element_type=jnp.float32)
        inner_grad = jnp.dot(branch_low, downweight.T, preferred_element_type=jnp.float32) * gelu_slope
        upbias_grad = lax.optimization_barrier(jnp.sum(inner_grad, axis=0))
        inner_low = inner_grad.astype(jnp.bfloat16)
        upweight_grad = jnp.dot(act_two.T, inner_low, preferred_element_type=jnp.float32)
        acttwo_grad = jnp.dot(inner_low, upweight.T, preferred_element_type=jnp.float32)
        mlpgain_grad = lax.optimization_barrier(jnp.sum(acttwo_grad * normed_two, axis=0))
        mlpshift_grad = lax.optimization_barrier(jnp.sum(acttwo_grad, axis=0))
        middle_grad = out_grad + norm_backward(acttwo_grad * gain_two, normed_two, spread_two)
        attnscale_grad = lax.optimization_barrier(jnp.sum(middle_grad * branch_one, axis=0))
        branchone_grad = middle_grad * scale_one
        projbias_grad = lax.optimization_barrier(jnp.sum(branchone_grad, axis=0))
        proj_low = branchone_grad.astype(jnp.bfloat16)
        projweight_grad = jnp.dot(attended.T, proj_low, preferred_element_type=jnp.float32)
        attn_back = jnp.dot(proj_low, projweight.T, preferred_element_type=jnp.float32).astype(jnp.bfloat16)
        back_heads = split_heads(attn_back)
        prob_grad = jnp.einsum('qhe,khe->hqk', back_heads, value_heads)
        row_dot = lax.optimization_barrier(jnp.sum(probs * prob_grad, axis=-1, keepdims=True))
        score_low = (probs * (prob_grad - row_dot)).astype(jnp.bfloat16).astype(jnp.float32)
        query_grad = (jnp.einsum('hqk,khe->qhe', score_low, key_heads) * SCORE_SCALE).reshape(LEN, D)
        key_grad = (jnp.einsum('hqk,qhe->khe', score_low, query_heads) * SCORE_SCALE).reshape(LEN, D)
        value_grad = jnp.einsum('hqk,qhe->khe', prob_low.astype(jnp.float32), back_heads).reshape(LEN, D)
        querybias_grad = lax.optimization_barrier(jnp.sum(query_grad, axis=0))
        valuebias_grad = lax.optimization_barrier(jnp.sum(value_grad, axis=0))
        mixed_low = jnp.concatenate([query_grad, key_grad, value_grad], axis=1).astype(jnp.bfloat16)
        qkvweight_grad = jnp.dot(act_one.T, mixed_low, preferred_element_type=jnp.float32)
        actone_grad = jnp.dot(mixed_low, qkvweight.T, preferred_element_type=jnp.float32)
        attngain_grad = lax.optimization_barrier(jnp.sum(actone_grad * normed_one, axis=0))
        attnshift_grad = lax.optimization_barrier(jnp.sum(actone_grad, axis=0))
        tokens_grad = middle_grad + norm_backward(actone_grad * gain_one, normed_one, spread_one)
        grads = (attngain_grad, attnshift_grad, qkvweight_grad, querybias_grad, valuebias_grad, projweight_grad, projbias_grad, attnscale_grad, mlpgain_grad, mlpshift_grad, upweight_grad, upbias_grad, downweight_grad, downbias_grad, mlpscale_grad)
        updated = tuple((running + addend for running, addend in zip(totals, grads)))
        return (updated, (block_out, tokens_grad))
    extents = ((D,), (D,), (D, 3 * D), (D,), (D,), (D, D), (D,), (D,), (D,), (D,), (D, FF), (FF,), (FF, D), (D,), (D,))
    initial = tuple((jnp.zeros(extent, jnp.float32) for extent in extents))
    finals, outputs = lax.scan(image_step, initial, (tokens, key_valid, cotangent))
    return (outputs[0], outputs[1], finals[0], finals[1], finals[2], finals[3], finals[4], finals[5], finals[6], finals[7], finals[8], finals[9], finals[10], finals[11], finals[12], finals[13], finals[14])
```

```python
import functools

import jax
import jax.numpy as jnp
from jax import lax
from jax.sharding import PartitionSpec as P

HEADS = 16
HEAD = 64


EPSILON = 1e-06
SCORE_SCALE = 0.125
ROOT_HALF = 0.7071067811865476
INV_ROOT_TAU = 0.3989422804014327
MASKED = -1e30


def norm_forward(hidden):
    center = hidden - jnp.mean(hidden, axis=-1, keepdims=True)
    spread = lax.rsqrt(jnp.mean(center * center, axis=-1, keepdims=True) + EPSILON)
    return (center * spread, spread)


def norm_backward(grad_norm, normed, spread):
    first_mean = jnp.mean(grad_norm, axis=-1, keepdims=True)
    second_mean = jnp.mean(grad_norm * normed, axis=-1, keepdims=True)
    return spread * (grad_norm - first_mean - normed * second_mean)


def gelu_pair(hidden):
    cumulative = 0.5 * (1.0 + lax.erf(hidden * ROOT_HALF))
    gelu_slope = cumulative + hidden * jnp.exp(-0.5 * hidden * hidden) * INV_ROOT_TAU
    return (hidden * cumulative, gelu_slope)


def split_heads(matrix, images):
    return matrix.reshape(images, -1, HEADS, HEAD)


def score_block(query_heads, key_heads, key_valid):
    scores = (
        jnp.einsum("iqhe,ikhe->ihqk", query_heads, key_heads, preferred_element_type=jnp.float32)
        * SCORE_SCALE
    )
    return jnp.where((key_valid > 0)[:, None, None, :], scores, MASKED)


def contract_rows(left, right):
    return lax.dot_general(
        left, right, (((0,), (0,)), ((), ())), preferred_element_type=jnp.float32
    )


def times_transposed(left, weight):
    return lax.dot_general(
        left, weight, (((1,), (1,)), ((), ())), preferred_element_type=jnp.float32
    )


def per_device(
    tokens,
    key_valid,
    cotangent,
    attngain,
    attnshift,
    qkvweight,
    querybias,
    valuebias,
    projweight,
    projbias,
    attnscale,
    mlpgain,
    mlpshift,
    upweight,
    upbias,
    downweight,
    downbias,
    mlpscale,
):
    images, tok_rows, feat_width = tokens.shape
    total_rows = images * tok_rows
    gain_one, shift_one, qkv_full, qbias_full, vbias_full, proj_full, pbias_full, scale_one = (
        lax.all_gather(attngain, ("shard", "seq"), axis=0, tiled=True),
        lax.all_gather(attnshift, ("shard", "seq"), axis=0, tiled=True),
        lax.all_gather(qkvweight, ("shard", "seq"), axis=0, tiled=True),
        lax.all_gather(querybias, ("shard", "seq"), axis=0, tiled=True),
        lax.all_gather(valuebias, ("shard", "seq"), axis=0, tiled=True),
        lax.all_gather(projweight, ("shard", "seq"), axis=0, tiled=True),
        lax.all_gather(projbias, ("shard", "seq"), axis=0, tiled=True),
        lax.all_gather(attnscale, ("shard", "seq"), axis=0, tiled=True),
    )
    hidden = tokens.reshape(total_rows, feat_width).astype(jnp.float32)
    normed_one, spread_one = norm_forward(hidden)
    act_one = (normed_one * gain_one.astype(jnp.float32) + shift_one.astype(jnp.float32)).astype(
        jnp.bfloat16
    )
    mixed = jnp.dot(act_one, qkv_full, preferred_element_type=jnp.float32)
    queries = (mixed[:, :feat_width] + qbias_full.astype(jnp.float32)).astype(jnp.bfloat16)
    key_local = (
        mixed[:, feat_width : 2 * feat_width]
        .astype(jnp.bfloat16)
        .reshape(images, tok_rows, feat_width)
    )
    value_local = (
        (mixed[:, 2 * feat_width :] + vbias_full.astype(jnp.float32))
        .astype(jnp.bfloat16)
        .reshape(images, tok_rows, feat_width)
    )
    key_all, value_all = (
        lax.all_gather(key_local, "seq", axis=1, tiled=True),
        lax.all_gather(value_local, "seq", axis=1, tiled=True),
    )
    query_heads = split_heads(queries, images)
    key_heads = split_heads(key_all, images)
    value_heads = split_heads(value_all, images)
    scores = score_block(query_heads, key_heads, key_valid)
    top_score = jnp.max(scores, axis=-1, keepdims=True)
    log_total = top_score + jnp.log(jnp.sum(jnp.exp(scores - top_score), axis=-1, keepdims=True))
    prob_low = jnp.exp(scores - log_total).astype(jnp.bfloat16)
    attended = (
        jnp.einsum("ihqk,ikhe->iqhe", prob_low, value_heads, preferred_element_type=jnp.float32)
        .reshape(total_rows, feat_width)
        .astype(jnp.bfloat16)
    )
    branch_one = jnp.dot(
        attended, proj_full, preferred_element_type=jnp.float32
    ) + pbias_full.astype(jnp.float32)
    middle = hidden + scale_one.astype(jnp.float32) * branch_one
    gain_two, shift_two, up_full, upb_full, down_full, downb_full, scale_two = (
        lax.all_gather(mlpgain, ("shard", "seq"), axis=0, tiled=True),
        lax.all_gather(mlpshift, ("shard", "seq"), axis=0, tiled=True),
        lax.all_gather(upweight, ("shard", "seq"), axis=0, tiled=True),
        lax.all_gather(upbias, ("shard", "seq"), axis=0, tiled=True),
        lax.all_gather(downweight, ("shard", "seq"), axis=0, tiled=True),
        lax.all_gather(downbias, ("shard", "seq"), axis=0, tiled=True),
        lax.all_gather(mlpscale, ("shard", "seq"), axis=0, tiled=True),
    )
    normed_two, spread_two = norm_forward(middle)
    act_two = (normed_two * gain_two.astype(jnp.float32) + shift_two.astype(jnp.float32)).astype(
        jnp.bfloat16
    )
    inner_pre = jnp.dot(act_two, up_full, preferred_element_type=jnp.float32) + upb_full.astype(
        jnp.float32
    )
    activated, gelu_slope = gelu_pair(inner_pre)
    act_three = activated.astype(jnp.bfloat16)
    branch_two = jnp.dot(
        act_three, down_full, preferred_element_type=jnp.float32
    ) + downb_full.astype(jnp.float32)
    block_out = middle + scale_two.astype(jnp.float32) * branch_two
    out_grad = cotangent.reshape(total_rows, feat_width).astype(jnp.float32)
    mlpscale_grad = jnp.sum(out_grad * branch_two, axis=0)
    branch_grad = out_grad * scale_two.astype(jnp.float32)
    downbias_grad = jnp.sum(branch_grad, axis=0)
    branch_low = branch_grad.astype(jnp.bfloat16)
    downweight_grad = contract_rows(act_three, branch_low)
    inner_grad = times_transposed(branch_low, down_full) * gelu_slope
    upbias_grad = jnp.sum(inner_grad, axis=0)
    inner_low = inner_grad.astype(jnp.bfloat16)
    upweight_grad = contract_rows(act_two, inner_low)
    acttwo_grad = times_transposed(inner_low, up_full)
    mlpgain_grad = jnp.sum(acttwo_grad * normed_two, axis=0)
    mlpshift_grad = jnp.sum(acttwo_grad, axis=0)
    middle_grad = out_grad + norm_backward(
        acttwo_grad * gain_two.astype(jnp.float32), normed_two, spread_two
    )
    mlp_part = (
        lax.psum_scatter(mlpgain_grad, ("shard", "seq"), scatter_dimension=0, tiled=True),
        lax.psum_scatter(mlpshift_grad, ("shard", "seq"), scatter_dimension=0, tiled=True),
        lax.psum_scatter(upweight_grad, ("shard", "seq"), scatter_dimension=0, tiled=True),
        lax.psum_scatter(upbias_grad, ("shard", "seq"), scatter_dimension=0, tiled=True),
        lax.psum_scatter(downweight_grad, ("shard", "seq"), scatter_dimension=0, tiled=True),
        lax.psum_scatter(downbias_grad, ("shard", "seq"), scatter_dimension=0, tiled=True),
        lax.psum_scatter(mlpscale_grad, ("shard", "seq"), scatter_dimension=0, tiled=True),
    )
    mlp_total = lax.psum(
        (mlp_part[0], mlp_part[1], mlp_part[2], mlp_part[3], mlp_part[4], mlp_part[5], mlp_part[6]),
        "rep",
    )
    attnscale_grad = jnp.sum(middle_grad * branch_one, axis=0)
    branchone_grad = middle_grad * scale_one.astype(jnp.float32)
    projbias_grad = jnp.sum(branchone_grad, axis=0)
    proj_low = branchone_grad.astype(jnp.bfloat16)
    projweight_grad = contract_rows(attended, proj_low)
    attn_back = times_transposed(proj_low, proj_full).astype(jnp.bfloat16)
    back_heads = split_heads(attn_back, images)
    scores = score_block(query_heads, key_heads, key_valid)
    probs = jnp.exp(scores - log_total)
    prob_low = probs.astype(jnp.bfloat16)
    prob_grad = jnp.einsum(
        "iqhe,ikhe->ihqk", back_heads, value_heads, preferred_element_type=jnp.float32
    )
    row_dot = jnp.sum(probs * prob_grad, axis=-1, keepdims=True)
    score_low = (probs * (prob_grad - row_dot)).astype(jnp.bfloat16)
    query_grad = (
        jnp.einsum("ihqk,ikhe->iqhe", score_low, key_heads, preferred_element_type=jnp.float32)
        * SCORE_SCALE
    ).reshape(total_rows, feat_width)
    key_part = (
        jnp.einsum("ihqk,iqhe->ikhe", score_low, query_heads, preferred_element_type=jnp.float32)
        * SCORE_SCALE
    ).reshape(images, -1, feat_width)
    value_part = jnp.einsum(
        "ihqk,iqhe->ikhe", prob_low, back_heads, preferred_element_type=jnp.float32
    ).reshape(images, -1, feat_width)
    key_grad, value_grad = (
        lax.psum_scatter(key_part, "seq", scatter_dimension=1, tiled=True),
        lax.psum_scatter(value_part, "seq", scatter_dimension=1, tiled=True),
    )
    key_grad = key_grad.reshape(total_rows, feat_width)
    value_grad = value_grad.reshape(total_rows, feat_width)
    querybias_grad = jnp.sum(query_grad, axis=0)
    valuebias_grad = jnp.sum(value_grad, axis=0)
    mixed_low = jnp.concatenate([query_grad, key_grad, value_grad], axis=1).astype(jnp.bfloat16)
    qkvweight_grad = contract_rows(act_one, mixed_low)
    actone_grad = times_transposed(mixed_low, qkv_full)
    attngain_grad = jnp.sum(actone_grad * normed_one, axis=0)
    attnshift_grad = jnp.sum(actone_grad, axis=0)
    tokens_grad = middle_grad + norm_backward(
        actone_grad * gain_one.astype(jnp.float32), normed_one, spread_one
    )
    attn_part = (
        lax.psum_scatter(attngain_grad, ("shard", "seq"), scatter_dimension=0, tiled=True),
        lax.psum_scatter(attnshift_grad, ("shard", "seq"), scatter_dimension=0, tiled=True),
        lax.psum_scatter(qkvweight_grad, ("shard", "seq"), scatter_dimension=0, tiled=True),
        lax.psum_scatter(querybias_grad, ("shard", "seq"), scatter_dimension=0, tiled=True),
        lax.psum_scatter(valuebias_grad, ("shard", "seq"), scatter_dimension=0, tiled=True),
        lax.psum_scatter(projweight_grad, ("shard", "seq"), scatter_dimension=0, tiled=True),
        lax.psum_scatter(projbias_grad, ("shard", "seq"), scatter_dimension=0, tiled=True),
        lax.psum_scatter(attnscale_grad, ("shard", "seq"), scatter_dimension=0, tiled=True),
    )
    attn_total = lax.psum(
        (
            attn_part[0],
            attn_part[1],
            attn_part[2],
            attn_part[3],
            attn_part[4],
            attn_part[5],
            attn_part[6],
            attn_part[7],
        ),
        "rep",
    )
    return (
        block_out.reshape(images, tok_rows, feat_width),
        tokens_grad.reshape(images, tok_rows, feat_width),
        attn_total[0],
        attn_total[1],
        attn_total[2],
        attn_total[3],
        attn_total[4],
        attn_total[5],
        attn_total[6],
        attn_total[7],
        mlp_total[0],
        mlp_total[1],
        mlp_total[2],
        mlp_total[3],
        mlp_total[4],
        mlp_total[5],
        mlp_total[6],
    )


GROUP = ("shard", "seq")


def gather_rows(array):
    return lax.all_gather(array, GROUP, axis=0, tiled=True)


def scatter_rows(array):
    return lax.psum_scatter(
        array.astype(jnp.bfloat16), GROUP, scatter_dimension=0, tiled=True
    ).astype(jnp.float32)


def tensor_parallel(shards, seqs, *arguments):
    (
        tokens,
        key_valid,
        cotangent,
        attngain,
        attnshift,
        qkvweight,
        querybias,
        valuebias,
        projweight,
        projbias,
        attnscale,
        mlpgain,
        mlpshift,
        upweight,
        upbias,
        downweight,
        downbias,
        mlpscale,
    ) = arguments
    group = shards * seqs
    images, tok_rows, width = tokens.shape
    rows = images * tok_rows
    own = width // group
    length = key_valid.shape[1]
    group_images = shards * images
    own_heads = HEADS // group

    small = jnp.concatenate(
        [
            attngain,
            attnshift,
            projbias,
            attnscale,
            mlpgain,
            mlpshift,
            downbias,
            mlpscale,
            key_valid.reshape(-1).astype(jnp.bfloat16),
        ]
    )
    small_all = lax.all_gather(small, GROUP, axis=0, tiled=False)

    def vector(at):
        return small_all[:, at * own : (at + 1) * own].reshape(width).astype(jnp.float32)

    gain_one, shift_one, bias_proj, scale_one, gain_two, shift_two, bias_down, scale_two = [
        vector(at) for at in range(8)
    ]
    valid = small_all[:, 8 * own :].reshape(shards, seqs, images, length)[:, 0]
    valid = valid.reshape(group_images, length)

    def to_images(matrix):
        matrix = matrix.reshape(shards, seqs, images, tok_rows, own_heads, HEAD)
        return matrix.transpose(0, 2, 1, 3, 4, 5).reshape(group_images, length, own_heads, HEAD)

    def from_images(heads):
        heads = heads.reshape(shards, images, seqs, tok_rows, own)
        return heads.transpose(0, 2, 1, 3, 4).reshape(group * rows, own)

    def to_columns(weight, parts):
        split = weight.reshape(own, parts, group, -1)
        moved = lax.all_to_all(split, GROUP, split_axis=2, concat_axis=0, tiled=True)
        return moved.reshape(width, -1)

    def to_rows(grad, parts):
        split = grad.reshape(width, parts, 1, -1)
        moved = lax.all_to_all(split, GROUP, split_axis=0, concat_axis=2, tiled=True)
        return moved.reshape(own, -1)

    tokens_local = tokens.reshape(rows, width)
    tokens_all = gather_rows(tokens_local)
    qkv_own = to_columns(qkvweight, 3)
    up_own = to_columns(upweight, 1)
    cot_all = gather_rows(cotangent.reshape(rows, width))

    normed_one_all, _ = norm_forward(tokens_all.astype(jnp.float32))
    act_one = (normed_one_all * gain_one + shift_one).astype(jnp.bfloat16)
    mixed = jnp.dot(act_one, qkv_own, preferred_element_type=jnp.float32)
    query_heads = to_images((mixed[:, :own] + querybias.astype(jnp.float32)).astype(jnp.bfloat16))
    key_heads = to_images(mixed[:, own : 2 * own].astype(jnp.bfloat16))
    value_heads = to_images(
        (mixed[:, 2 * own :] + valuebias.astype(jnp.float32)).astype(jnp.bfloat16)
    )
    scores = score_block(query_heads, key_heads, valid)
    top_score = jnp.max(scores, axis=-1, keepdims=True)
    log_total = top_score + jnp.log(jnp.sum(jnp.exp(scores - top_score), axis=-1, keepdims=True))
    probs = jnp.exp(scores - log_total)
    prob_low = probs.astype(jnp.bfloat16)
    attended = from_images(
        jnp.einsum(
            "ihqk,ikhe->iqhe", prob_low, value_heads, preferred_element_type=jnp.float32
        ).astype(jnp.bfloat16)
    )
    branch_one = (
        scatter_rows(jnp.dot(attended, projweight, preferred_element_type=jnp.float32)) + bias_proj
    )
    hidden = tokens_local.astype(jnp.float32)
    normed_one, spread_one = norm_forward(hidden)
    middle = hidden + scale_one * branch_one
    normed_two, spread_two = norm_forward(middle)
    act_two = gather_rows((normed_two * gain_two + shift_two).astype(jnp.bfloat16))

    inner_pre = jnp.dot(act_two, up_own, preferred_element_type=jnp.float32) + upbias.astype(
        jnp.float32
    )
    activated, gelu_slope = gelu_pair(inner_pre)
    act_three = activated.astype(jnp.bfloat16)
    branch_low = (cot_all.astype(jnp.float32) * scale_two).astype(jnp.bfloat16)
    inner_grad = times_transposed(branch_low, downweight) * gelu_slope
    inner_low = inner_grad.astype(jnp.bfloat16)
    acttwo_grad = scatter_rows(times_transposed(inner_low, up_own))
    branch_two = (
        scatter_rows(jnp.dot(act_three, downweight, preferred_element_type=jnp.float32)) + bias_down
    )
    upbias_grad = jnp.sum(inner_grad, axis=0)
    downweight_grad = contract_rows(act_three, branch_low).astype(jnp.bfloat16)
    upweight_grad = contract_rows(act_two, inner_low).astype(jnp.bfloat16)
    out_grad = cotangent.reshape(rows, width).astype(jnp.float32)
    middle_grad = out_grad + norm_backward(acttwo_grad * gain_two, normed_two, spread_two)
    branchone_grad = middle_grad * scale_one
    proj_low = gather_rows(branchone_grad.astype(jnp.bfloat16))

    block_out = middle + scale_two * branch_two

    back_heads = to_images(times_transposed(proj_low, projweight).astype(jnp.bfloat16))
    projweight_grad = contract_rows(attended, proj_low).astype(jnp.bfloat16)
    prob_grad = jnp.einsum(
        "iqhe,ikhe->ihqk", back_heads, value_heads, preferred_element_type=jnp.float32
    )
    row_dot = jnp.sum(probs * prob_grad, axis=-1, keepdims=True)
    score_low = (probs * (prob_grad - row_dot)).astype(jnp.bfloat16)
    query_grad = from_images(
        jnp.einsum("ihqk,ikhe->iqhe", score_low, key_heads, preferred_element_type=jnp.float32)
        * SCORE_SCALE
    )
    key_grad = from_images(
        jnp.einsum("ihqk,iqhe->ikhe", score_low, query_heads, preferred_element_type=jnp.float32)
        * SCORE_SCALE
    )
    value_grad = from_images(
        jnp.einsum("ihqk,iqhe->ikhe", prob_low, back_heads, preferred_element_type=jnp.float32)
    )
    mixed_low = jnp.concatenate([query_grad, key_grad, value_grad], axis=1).astype(jnp.bfloat16)
    actone_part = times_transposed(mixed_low, qkv_own)
    actone_grad = scatter_rows(actone_part)
    qkvweight_grad = contract_rows(act_one, mixed_low).astype(jnp.bfloat16)
    tokens_grad = middle_grad + norm_backward(actone_grad * gain_one, normed_one, spread_one)

    vectors = jnp.stack(
        [
            jnp.sum(actone_part * normed_one_all, axis=0),
            jnp.sum(actone_part, axis=0),
            jnp.sum(branchone_grad, axis=0),
            jnp.sum(middle_grad * branch_one, axis=0),
            jnp.sum(acttwo_grad * normed_two, axis=0),
            jnp.sum(acttwo_grad, axis=0),
            jnp.sum(out_grad * scale_two, axis=0),
            jnp.sum(out_grad * branch_two, axis=0),
        ]
    )
    place = lax.axis_index(GROUP)
    biases = jnp.concatenate(
        [jnp.sum(query_grad, axis=0), jnp.sum(value_grad, axis=0), upbias_grad]
    ).reshape(-1)
    bias_slots = lax.dynamic_update_slice(
        jnp.zeros((group, biases.shape[0]), jnp.float32), biases[None], (place, 0)
    )
    totals = lax.psum(
        jnp.concatenate([vectors.reshape(-1), bias_slots.reshape(-1)]), ("rep",) + GROUP
    )
    vectors = totals[: 8 * width].reshape(8, width)
    vectors = lax.dynamic_slice(vectors, (0, place * own), (8, own))
    biases = lax.dynamic_slice(
        totals[8 * width :].reshape(group, -1), (place, 0), (1, biases.shape[0])
    )[0]

    downweight_grad, upweight_grad = lax.psum((downweight_grad, upweight_grad), "rep")
    upweight_grad = to_rows(upweight_grad, 1)
    upweight_grad, projweight_grad, qkvweight_grad = lax.optimization_barrier(
        (upweight_grad, projweight_grad, qkvweight_grad)
    )
    projweight_grad, qkvweight_grad = lax.psum((projweight_grad, qkvweight_grad), "rep")
    qkvweight_grad = to_rows(qkvweight_grad, 3)

    return (
        block_out.reshape(images, tok_rows, width),
        tokens_grad.reshape(images, tok_rows, width),
        vectors[0],
        vectors[1],
        qkvweight_grad.astype(jnp.float32),
        biases[:own],
        biases[own : 2 * own],
        projweight_grad.astype(jnp.float32),
        vectors[2],
        vectors[3],
        vectors[4],
        vectors[5],
        upweight_grad.astype(jnp.float32),
        biases[2 * own :],
        downweight_grad.astype(jnp.float32),
        vectors[6],
        vectors[7],
    )


def solution(mesh):
    shards, seqs = mesh.shape["shard"], mesh.shape["seq"]
    if HEADS % (shards * seqs) == 0:
        body = functools.partial(tensor_parallel, shards, seqs)
    else:
        body = per_device
    return jax.shard_map(
        body,
        mesh=mesh,
        in_specs=(
            P(("rep", "shard"), "seq", None),
            P(("rep", "shard"), None),
            P(("rep", "shard"), "seq", None),
            P(("shard", "seq")),
            P(("shard", "seq")),
            P(("shard", "seq"), None),
            P(("shard", "seq")),
            P(("shard", "seq")),
            P(("shard", "seq"), None),
            P(("shard", "seq")),
            P(("shard", "seq")),
            P(("shard", "seq")),
            P(("shard", "seq")),
            P(("shard", "seq"), None),
            P(("shard", "seq")),
            P(("shard", "seq"), None),
            P(("shard", "seq")),
            P(("shard", "seq")),
        ),
        out_specs=(
            P(("rep", "shard"), "seq", None),
            P(("rep", "shard"), "seq", None),
            P(("shard", "seq")),
            P(("shard", "seq")),
            P(("shard", "seq"), None),
            P(("shard", "seq")),
            P(("shard", "seq")),
            P(("shard", "seq"), None),
            P(("shard", "seq")),
            P(("shard", "seq")),
            P(("shard", "seq")),
            P(("shard", "seq")),
            P(("shard", "seq"), None),
            P(("shard", "seq")),
            P(("shard", "seq"), None),
            P(("shard", "seq")),
            P(("shard", "seq")),
        ),
        check_vma=False,
    )
```

```python
import functools

import jax
import jax.numpy as jnp
from jax import lax
from jax.experimental import pallas as pl
from jax.experimental.pallas import tpu as pltpu
from jax.sharding import PartitionSpec as P

HEADS = 16
HEAD = 64


EPSILON = 1e-06
SCORE_SCALE = 0.125
ROOT_HALF = 0.7071067811865476
INV_ROOT_TAU = 0.3989422804014327
MASKED = -1e30


def norm_forward(hidden):
    center = hidden - jnp.mean(hidden, axis=-1, keepdims=True)
    spread = lax.rsqrt(jnp.mean(center * center, axis=-1, keepdims=True) + EPSILON)
    return (center * spread, spread)


def norm_backward(grad_norm, normed, spread):
    first_mean = jnp.mean(grad_norm, axis=-1, keepdims=True)
    second_mean = jnp.mean(grad_norm * normed, axis=-1, keepdims=True)
    return spread * (grad_norm - first_mean - normed * second_mean)


def gelu_pair(hidden):
    cumulative = 0.5 * (1.0 + lax.erf(hidden * ROOT_HALF))
    gelu_slope = cumulative + hidden * jnp.exp(-0.5 * hidden * hidden) * INV_ROOT_TAU
    return (hidden * cumulative, gelu_slope)


def split_heads(matrix, images):
    return matrix.reshape(images, -1, HEADS, HEAD)


def score_block(query_heads, key_heads, key_valid):
    scores = (
        jnp.einsum("iqhe,ikhe->ihqk", query_heads, key_heads, preferred_element_type=jnp.float32)
        * SCORE_SCALE
    )
    return jnp.where((key_valid > 0)[:, None, None, :], scores, MASKED)


def contract_rows(left, right):
    return lax.dot_general(
        left, right, (((0,), (0,)), ((), ())), preferred_element_type=jnp.float32
    )


def times_transposed(left, weight):
    return lax.dot_general(
        left, weight, (((1,), (1,)), ((), ())), preferred_element_type=jnp.float32
    )


def per_device(
    tokens,
    key_valid,
    cotangent,
    attngain,
    attnshift,
    qkvweight,
    querybias,
    valuebias,
    projweight,
    projbias,
    attnscale,
    mlpgain,
    mlpshift,
    upweight,
    upbias,
    downweight,
    downbias,
    mlpscale,
):
    images, tok_rows, feat_width = tokens.shape
    total_rows = images * tok_rows
    gain_one, shift_one, qkv_full, qbias_full, vbias_full, proj_full, pbias_full, scale_one = (
        lax.all_gather(attngain, ("shard", "seq"), axis=0, tiled=True),
        lax.all_gather(attnshift, ("shard", "seq"), axis=0, tiled=True),
        lax.all_gather(qkvweight, ("shard", "seq"), axis=0, tiled=True),
        lax.all_gather(querybias, ("shard", "seq"), axis=0, tiled=True),
        lax.all_gather(valuebias, ("shard", "seq"), axis=0, tiled=True),
        lax.all_gather(projweight, ("shard", "seq"), axis=0, tiled=True),
        lax.all_gather(projbias, ("shard", "seq"), axis=0, tiled=True),
        lax.all_gather(attnscale, ("shard", "seq"), axis=0, tiled=True),
    )
    hidden = tokens.reshape(total_rows, feat_width).astype(jnp.float32)
    normed_one, spread_one = norm_forward(hidden)
    act_one = (normed_one * gain_one.astype(jnp.float32) + shift_one.astype(jnp.float32)).astype(
        jnp.bfloat16
    )
    mixed = jnp.dot(act_one, qkv_full, preferred_element_type=jnp.float32)
    queries = (mixed[:, :feat_width] + qbias_full.astype(jnp.float32)).astype(jnp.bfloat16)
    key_local = (
        mixed[:, feat_width : 2 * feat_width]
        .astype(jnp.bfloat16)
        .reshape(images, tok_rows, feat_width)
    )
    value_local = (
        (mixed[:, 2 * feat_width :] + vbias_full.astype(jnp.float32))
        .astype(jnp.bfloat16)
        .reshape(images, tok_rows, feat_width)
    )
    key_all, value_all = (
        lax.all_gather(key_local, "seq", axis=1, tiled=True),
        lax.all_gather(value_local, "seq", axis=1, tiled=True),
    )
    query_heads = split_heads(queries, images)
    key_heads = split_heads(key_all, images)
    value_heads = split_heads(value_all, images)
    scores = score_block(query_heads, key_heads, key_valid)
    top_score = jnp.max(scores, axis=-1, keepdims=True)
    log_total = top_score + jnp.log(jnp.sum(jnp.exp(scores - top_score), axis=-1, keepdims=True))
    prob_low = jnp.exp(scores - log_total).astype(jnp.bfloat16)
    attended = (
        jnp.einsum("ihqk,ikhe->iqhe", prob_low, value_heads, preferred_element_type=jnp.float32)
        .reshape(total_rows, feat_width)
        .astype(jnp.bfloat16)
    )
    branch_one = jnp.dot(
        attended, proj_full, preferred_element_type=jnp.float32
    ) + pbias_full.astype(jnp.float32)
    middle = hidden + scale_one.astype(jnp.float32) * branch_one
    gain_two, shift_two, up_full, upb_full, down_full, downb_full, scale_two = (
        lax.all_gather(mlpgain, ("shard", "seq"), axis=0, tiled=True),
        lax.all_gather(mlpshift, ("shard", "seq"), axis=0, tiled=True),
        lax.all_gather(upweight, ("shard", "seq"), axis=0, tiled=True),
        lax.all_gather(upbias, ("shard", "seq"), axis=0, tiled=True),
        lax.all_gather(downweight, ("shard", "seq"), axis=0, tiled=True),
        lax.all_gather(downbias, ("shard", "seq"), axis=0, tiled=True),
        lax.all_gather(mlpscale, ("shard", "seq"), axis=0, tiled=True),
    )
    normed_two, spread_two = norm_forward(middle)
    act_two = (normed_two * gain_two.astype(jnp.float32) + shift_two.astype(jnp.float32)).astype(
        jnp.bfloat16
    )
    inner_pre = jnp.dot(act_two, up_full, preferred_element_type=jnp.float32) + upb_full.astype(
        jnp.float32
    )
    activated, gelu_slope = gelu_pair(inner_pre)
    act_three = activated.astype(jnp.bfloat16)
    branch_two = jnp.dot(
        act_three, down_full, preferred_element_type=jnp.float32
    ) + downb_full.astype(jnp.float32)
    block_out = middle + scale_two.astype(jnp.float32) * branch_two
    out_grad = cotangent.reshape(total_rows, feat_width).astype(jnp.float32)
    mlpscale_grad = jnp.sum(out_grad * branch_two, axis=0)
    branch_grad = out_grad * scale_two.astype(jnp.float32)
    downbias_grad = jnp.sum(branch_grad, axis=0)
    branch_low = branch_grad.astype(jnp.bfloat16)
    downweight_grad = contract_rows(act_three, branch_low)
    inner_grad = times_transposed(branch_low, down_full) * gelu_slope
    upbias_grad = jnp.sum(inner_grad, axis=0)
    inner_low = inner_grad.astype(jnp.bfloat16)
    upweight_grad = contract_rows(act_two, inner_low)
    acttwo_grad = times_transposed(inner_low, up_full)
    mlpgain_grad = jnp.sum(acttwo_grad * normed_two, axis=0)
    mlpshift_grad = jnp.sum(acttwo_grad, axis=0)
    middle_grad = out_grad + norm_backward(
        acttwo_grad * gain_two.astype(jnp.float32), normed_two, spread_two
    )
    mlp_part = (
        lax.psum_scatter(mlpgain_grad, ("shard", "seq"), scatter_dimension=0, tiled=True),
        lax.psum_scatter(mlpshift_grad, ("shard", "seq"), scatter_dimension=0, tiled=True),
        lax.psum_scatter(upweight_grad, ("shard", "seq"), scatter_dimension=0, tiled=True),
        lax.psum_scatter(upbias_grad, ("shard", "seq"), scatter_dimension=0, tiled=True),
        lax.psum_scatter(downweight_grad, ("shard", "seq"), scatter_dimension=0, tiled=True),
        lax.psum_scatter(downbias_grad, ("shard", "seq"), scatter_dimension=0, tiled=True),
        lax.psum_scatter(mlpscale_grad, ("shard", "seq"), scatter_dimension=0, tiled=True),
    )
    mlp_total = lax.psum(
        (mlp_part[0], mlp_part[1], mlp_part[2], mlp_part[3], mlp_part[4], mlp_part[5], mlp_part[6]),
        "rep",
    )
    attnscale_grad = jnp.sum(middle_grad * branch_one, axis=0)
    branchone_grad = middle_grad * scale_one.astype(jnp.float32)
    projbias_grad = jnp.sum(branchone_grad, axis=0)
    proj_low = branchone_grad.astype(jnp.bfloat16)
    projweight_grad = contract_rows(attended, proj_low)
    attn_back = times_transposed(proj_low, proj_full).astype(jnp.bfloat16)
    back_heads = split_heads(attn_back, images)
    scores = score_block(query_heads, key_heads, key_valid)
    probs = jnp.exp(scores - log_total)
    prob_low = probs.astype(jnp.bfloat16)
    prob_grad = jnp.einsum(
        "iqhe,ikhe->ihqk", back_heads, value_heads, preferred_element_type=jnp.float32
    )
    row_dot = jnp.sum(probs * prob_grad, axis=-1, keepdims=True)
    score_low = (probs * (prob_grad - row_dot)).astype(jnp.bfloat16)
    query_grad = (
        jnp.einsum("ihqk,ikhe->iqhe", score_low, key_heads, preferred_element_type=jnp.float32)
        * SCORE_SCALE
    ).reshape(total_rows, feat_width)
    key_part = (
        jnp.einsum("ihqk,iqhe->ikhe", score_low, query_heads, preferred_element_type=jnp.float32)
        * SCORE_SCALE
    ).reshape(images, -1, feat_width)
    value_part = jnp.einsum(
        "ihqk,iqhe->ikhe", prob_low, back_heads, preferred_element_type=jnp.float32
    ).reshape(images, -1, feat_width)
    key_grad, value_grad = (
        lax.psum_scatter(key_part, "seq", scatter_dimension=1, tiled=True),
        lax.psum_scatter(value_part, "seq", scatter_dimension=1, tiled=True),
    )
    key_grad = key_grad.reshape(total_rows, feat_width)
    value_grad = value_grad.reshape(total_rows, feat_width)
    querybias_grad = jnp.sum(query_grad, axis=0)
    valuebias_grad = jnp.sum(value_grad, axis=0)
    mixed_low = jnp.concatenate([query_grad, key_grad, value_grad], axis=1).astype(jnp.bfloat16)
    qkvweight_grad = contract_rows(act_one, mixed_low)
    actone_grad = times_transposed(mixed_low, qkv_full)
    attngain_grad = jnp.sum(actone_grad * normed_one, axis=0)
    attnshift_grad = jnp.sum(actone_grad, axis=0)
    tokens_grad = middle_grad + norm_backward(
        actone_grad * gain_one.astype(jnp.float32), normed_one, spread_one
    )
    attn_part = (
        lax.psum_scatter(attngain_grad, ("shard", "seq"), scatter_dimension=0, tiled=True),
        lax.psum_scatter(attnshift_grad, ("shard", "seq"), scatter_dimension=0, tiled=True),
        lax.psum_scatter(qkvweight_grad, ("shard", "seq"), scatter_dimension=0, tiled=True),
        lax.psum_scatter(querybias_grad, ("shard", "seq"), scatter_dimension=0, tiled=True),
        lax.psum_scatter(valuebias_grad, ("shard", "seq"), scatter_dimension=0, tiled=True),
        lax.psum_scatter(projweight_grad, ("shard", "seq"), scatter_dimension=0, tiled=True),
        lax.psum_scatter(projbias_grad, ("shard", "seq"), scatter_dimension=0, tiled=True),
        lax.psum_scatter(attnscale_grad, ("shard", "seq"), scatter_dimension=0, tiled=True),
    )
    attn_total = lax.psum(
        (
            attn_part[0],
            attn_part[1],
            attn_part[2],
            attn_part[3],
            attn_part[4],
            attn_part[5],
            attn_part[6],
            attn_part[7],
        ),
        "rep",
    )
    return (
        block_out.reshape(images, tok_rows, feat_width),
        tokens_grad.reshape(images, tok_rows, feat_width),
        attn_total[0],
        attn_total[1],
        attn_total[2],
        attn_total[3],
        attn_total[4],
        attn_total[5],
        attn_total[6],
        attn_total[7],
        mlp_total[0],
        mlp_total[1],
        mlp_total[2],
        mlp_total[3],
        mlp_total[4],
        mlp_total[5],
        mlp_total[6],
    )


GROUP = ("shard", "seq")


def gather_rows(array):
    return lax.all_gather(array, GROUP, axis=0, tiled=True)


VMEM_LIMIT = 40 * 1024 * 1024


def chip_barrier(shards, shard, other):
    barrier = pltpu.get_barrier_semaphore()
    for step in range(1, shards):
        pl.semaphore_signal(
            barrier, inc=1, device_id={"shard": lax.rem(shard + step, shards)}
        )
    pl.semaphore_signal(barrier, inc=1, device_id={"seq": other})
    pl.semaphore_wait(barrier, shards)


def gather_kernel(shards, count, *refs):
    sources, results = refs[:count], refs[count : 2 * count]
    send_sem, recv_sem, local_sem = refs[2 * count :]
    shard, seq = lax.axis_index("shard"), lax.axis_index("seq")
    other = 1 - seq
    place = 2 * shard + seq
    chip_barrier(shards, shard, other)

    def push(source, target, slot, device):
        copy = pltpu.make_async_remote_copy(
            src_ref=source,
            dst_ref=target,
            send_sem=send_sem.at[slot],
            recv_sem=recv_sem.at[slot],
            device_id=device,
        )
        copy.start()
        return copy

    slots = 2 * shards - 1
    along, pending, local = {}, [], []
    for at in range(count):
        for step in range(1, shards):
            along[at, step] = push(
                sources[at],
                results[at].at[place],
                at * slots + step - 1,
                {"shard": lax.rem(shard + step, shards)},
            )
        pending.append(
            push(sources[at], results[at].at[place], at * slots + shards - 1, {"seq": other})
        )
        copy = pltpu.make_async_copy(sources[at], results[at].at[place], local_sem.at[at])
        copy.start()
        local.append(copy)
    for at in range(count):
        for step in range(1, shards):
            along[at, step].wait_recv()
            origin = 2 * lax.rem(shard + shards - step, shards) + seq
            pending.append(
                push(
                    results[at].at[origin],
                    results[at].at[origin],
                    at * slots + shards - 1 + step,
                    {"seq": other},
                )
            )
    for copy in local:
        copy.wait()
    for copy in along.values():
        copy.wait_send()
    for copy in pending:
        copy.wait()


def gather_group(shards, call, *arrays):
    count = len(arrays)
    copies = count * (2 * shards - 1)
    results = pl.pallas_call(
        functools.partial(gather_kernel, shards, count),
        out_shape=[
            jax.ShapeDtypeStruct((2 * shards,) + array.shape, array.dtype) for array in arrays
        ],
        in_specs=[pl.BlockSpec(memory_space=pltpu.VMEM)] * count,
        out_specs=[pl.BlockSpec(memory_space=pltpu.VMEM)] * count,
        scratch_shapes=[
            pltpu.SemaphoreType.DMA((copies,)),
            pltpu.SemaphoreType.DMA((copies,)),
            pltpu.SemaphoreType.DMA((count,)),
        ],
        compiler_params=pltpu.CompilerParams(
            collective_id=call, has_side_effects=True, vmem_limit_bytes=VMEM_LIMIT
        ),
        name="gather_group_%d" % call,
    )(*arrays)
    return results


def scatter_kernel(shards, terms, total, near, outgoing, arrived, send_sem, recv_sem):
    shard, seq = lax.axis_index("shard"), lax.axis_index("seq")
    other = 1 - seq
    chip_barrier(shards, shard, other)

    def push(source, target, slot, device):
        copy = pltpu.make_async_remote_copy(
            src_ref=source,
            dst_ref=target,
            send_sem=send_sem.at[slot],
            recv_sem=recv_sem.at[slot],
            device_id=device,
        )
        copy.start()
        return copy

    first, second = [], []
    for step in range(1, shards + 1):
        target = lax.rem(shard + step, shards)
        first.append(
            push(terms.at[2 * target + other], near.at[step - 1], step - 1, {"seq": other})
        )
    for step in range(1, shards + 1):
        target = lax.rem(shard + step, shards)
        first[step - 1].wait_recv()
        both = terms[2 * target + seq].astype(jnp.float32) + near[step - 1].astype(jnp.float32)
        if step == shards:
            total[...] = both
        else:
            outgoing[step - 1] = both.astype(jnp.bfloat16)
            second.append(
                push(
                    outgoing.at[step - 1],
                    arrived.at[step - 1],
                    shards + step - 1,
                    {"shard": target},
                )
            )
    for step in range(1, shards):
        second[step - 1].wait_recv()
        total[...] += arrived[step - 1].astype(jnp.float32)
    for copy in first + second:
        copy.wait_send()


def scatter_group(shards, call, terms):
    terms = terms.astype(jnp.bfloat16)
    rows, columns = terms.shape
    block = (rows // (2 * shards), columns)
    copies = 2 * shards - 1
    return pl.pallas_call(
        functools.partial(scatter_kernel, shards),
        out_shape=jax.ShapeDtypeStruct(block, jnp.float32),
        in_specs=[pl.BlockSpec(memory_space=pltpu.VMEM)],
        out_specs=pl.BlockSpec(memory_space=pltpu.VMEM),
        scratch_shapes=[
            pltpu.VMEM((shards,) + block, jnp.bfloat16),
            pltpu.VMEM((shards - 1,) + block, jnp.bfloat16),
            pltpu.VMEM((shards - 1,) + block, jnp.bfloat16),
            pltpu.SemaphoreType.DMA((copies,)),
            pltpu.SemaphoreType.DMA((copies,)),
        ],
        compiler_params=pltpu.CompilerParams(
            collective_id=call, has_side_effects=True, vmem_limit_bytes=VMEM_LIMIT
        ),
        name="scatter_group_%d" % call,
    )(terms.reshape((2 * shards,) + block))


def tensor_parallel(shards, seqs, *arguments):
    (
        tokens,
        key_valid,
        cotangent,
        attngain,
        attnshift,
        qkvweight,
        querybias,
        valuebias,
        projweight,
        projbias,
        attnscale,
        mlpgain,
        mlpshift,
        upweight,
        upbias,
        downweight,
        downbias,
        mlpscale,
    ) = arguments
    group = shards * seqs
    images, tok_rows, width = tokens.shape
    rows = images * tok_rows
    own = width // group
    length = key_valid.shape[1]
    group_images = shards * images
    own_heads = HEADS // group

    small = jnp.concatenate(
        [
            attngain,
            attnshift,
            projbias,
            attnscale,
            mlpgain,
            mlpshift,
            downbias,
            mlpscale,
            key_valid.reshape(-1).astype(jnp.bfloat16),
        ]
    )
    used = small.shape[0]
    padded = -(-used // 2048) * 2048
    small = jnp.pad(small, (0, padded - used)).reshape(-1, 128)
    tokens_local = tokens.reshape(rows, width)
    tokens_all, small_all = gather_group(shards, 0, tokens_local, small)
    tokens_all = tokens_all.reshape(group * rows, width)
    small_all = small_all.reshape(group, padded)

    def vector(at):
        return small_all[:, at * own : (at + 1) * own].reshape(width).astype(jnp.float32)

    gain_one, shift_one, bias_proj, scale_one, gain_two, shift_two, bias_down, scale_two = [
        vector(at) for at in range(8)
    ]
    valid = small_all[:, 8 * own : used].reshape(shards, seqs, images, length)[:, 0]
    valid = valid.reshape(group_images, length)

    def to_images(matrix):
        matrix = matrix.reshape(shards, seqs, images, tok_rows, own_heads, HEAD)
        return matrix.transpose(0, 2, 1, 3, 4, 5).reshape(group_images, length, own_heads, HEAD)

    def from_images(heads):
        heads = heads.reshape(shards, images, seqs, tok_rows, own)
        return heads.transpose(0, 2, 1, 3, 4).reshape(group * rows, own)

    def to_columns(weight, parts):
        split = weight.reshape(own, parts, group, -1)
        moved = lax.all_to_all(split, GROUP, split_axis=2, concat_axis=0, tiled=True)
        return moved.reshape(width, -1)

    def to_rows(grad, parts):
        split = grad.reshape(width, parts, 1, -1)
        moved = lax.all_to_all(split, GROUP, split_axis=0, concat_axis=2, tiled=True)
        return moved.reshape(own, -1)

    qkv_own = to_columns(qkvweight, 3)
    up_own = to_columns(upweight, 1)
    cot_all = gather_rows(cotangent.reshape(rows, width))

    normed_one_all, _ = norm_forward(tokens_all.astype(jnp.float32))
    act_one = (normed_one_all * gain_one + shift_one).astype(jnp.bfloat16)
    mixed = jnp.dot(act_one, qkv_own, preferred_element_type=jnp.float32)
    query_heads = to_images((mixed[:, :own] + querybias.astype(jnp.float32)).astype(jnp.bfloat16))
    key_heads = to_images(mixed[:, own : 2 * own].astype(jnp.bfloat16))
    value_heads = to_images(
        (mixed[:, 2 * own :] + valuebias.astype(jnp.float32)).astype(jnp.bfloat16)
    )
    scores = score_block(query_heads, key_heads, valid)
    top_score = jnp.max(scores, axis=-1, keepdims=True)
    log_total = top_score + jnp.log(jnp.sum(jnp.exp(scores - top_score), axis=-1, keepdims=True))
    probs = jnp.exp(scores - log_total)
    prob_low = probs.astype(jnp.bfloat16)
    attended = from_images(
        jnp.einsum(
            "ihqk,ikhe->iqhe", prob_low, value_heads, preferred_element_type=jnp.float32
        ).astype(jnp.bfloat16)
    )
    branch_one = (
        scatter_group(shards, 1, jnp.dot(attended, projweight, preferred_element_type=jnp.float32)) + bias_proj
    )
    hidden = tokens_local.astype(jnp.float32)
    normed_one, spread_one = norm_forward(hidden)
    middle = hidden + scale_one * branch_one
    normed_two, spread_two = norm_forward(middle)
    act_two = gather_group(
        shards, 2, (normed_two * gain_two + shift_two).astype(jnp.bfloat16)
    )[0].reshape(group * rows, width)

    inner_pre = jnp.dot(act_two, up_own, preferred_element_type=jnp.float32) + upbias.astype(
        jnp.float32
    )
    activated, gelu_slope = gelu_pair(inner_pre)
    act_three = activated.astype(jnp.bfloat16)
    branch_low = (cot_all.astype(jnp.float32) * scale_two).astype(jnp.bfloat16)
    inner_grad = times_transposed(branch_low, downweight) * gelu_slope
    inner_low = inner_grad.astype(jnp.bfloat16)
    acttwo_grad = scatter_group(shards, 3, times_transposed(inner_low, up_own))
    branch_two = (
        scatter_group(shards, 4, jnp.dot(act_three, downweight, preferred_element_type=jnp.float32)) + bias_down
    )
    upbias_grad = jnp.sum(inner_grad, axis=0)
    downweight_grad = contract_rows(act_three, branch_low).astype(jnp.bfloat16)
    upweight_grad = contract_rows(act_two, inner_low).astype(jnp.bfloat16)
    out_grad = cotangent.reshape(rows, width).astype(jnp.float32)
    middle_grad = out_grad + norm_backward(acttwo_grad * gain_two, normed_two, spread_two)
    branchone_grad = middle_grad * scale_one
    proj_low = gather_group(shards, 5, branchone_grad.astype(jnp.bfloat16))[0].reshape(
        group * rows, width
    )

    block_out = middle + scale_two * branch_two

    back_heads = to_images(times_transposed(proj_low, projweight).astype(jnp.bfloat16))
    projweight_grad = contract_rows(attended, proj_low).astype(jnp.bfloat16)
    prob_grad = jnp.einsum(
        "iqhe,ikhe->ihqk", back_heads, value_heads, preferred_element_type=jnp.float32
    )
    row_dot = jnp.sum(probs * prob_grad, axis=-1, keepdims=True)
    score_low = (probs * (prob_grad - row_dot)).astype(jnp.bfloat16)
    query_grad = from_images(
        jnp.einsum("ihqk,ikhe->iqhe", score_low, key_heads, preferred_element_type=jnp.float32)
        * SCORE_SCALE
    )
    key_grad = from_images(
        jnp.einsum("ihqk,iqhe->ikhe", score_low, query_heads, preferred_element_type=jnp.float32)
        * SCORE_SCALE
    )
    value_grad = from_images(
        jnp.einsum("ihqk,iqhe->ikhe", prob_low, back_heads, preferred_element_type=jnp.float32)
    )
    mixed_low = jnp.concatenate([query_grad, key_grad, value_grad], axis=1).astype(jnp.bfloat16)
    actone_part = times_transposed(mixed_low, qkv_own)
    actone_grad = scatter_group(shards, 6, actone_part)
    qkvweight_grad = contract_rows(act_one, mixed_low).astype(jnp.bfloat16)
    tokens_grad = middle_grad + norm_backward(actone_grad * gain_one, normed_one, spread_one)

    vectors = jnp.stack(
        [
            jnp.sum(actone_part * normed_one_all, axis=0),
            jnp.sum(actone_part, axis=0),
            jnp.sum(branchone_grad, axis=0),
            jnp.sum(middle_grad * branch_one, axis=0),
            jnp.sum(acttwo_grad * normed_two, axis=0),
            jnp.sum(acttwo_grad, axis=0),
            jnp.sum(out_grad * scale_two, axis=0),
            jnp.sum(out_grad * branch_two, axis=0),
        ]
    )
    place = lax.axis_index(GROUP)
    biases = jnp.concatenate(
        [jnp.sum(query_grad, axis=0), jnp.sum(value_grad, axis=0), upbias_grad]
    ).reshape(-1)
    bias_slots = lax.dynamic_update_slice(
        jnp.zeros((group, biases.shape[0]), jnp.float32), biases[None], (place, 0)
    )
    totals = lax.psum(
        jnp.concatenate([vectors.reshape(-1), bias_slots.reshape(-1)]), ("rep",) + GROUP
    )
    vectors = totals[: 8 * width].reshape(8, width)
    vectors = lax.dynamic_slice(vectors, (0, place * own), (8, own))
    biases = lax.dynamic_slice(
        totals[8 * width :].reshape(group, -1), (place, 0), (1, biases.shape[0])
    )[0]

    downweight_grad, upweight_grad = lax.psum((downweight_grad, upweight_grad), "rep")
    upweight_grad = to_rows(upweight_grad, 1)
    upweight_grad, downweight_grad, projweight_grad, qkvweight_grad = lax.optimization_barrier(
        (upweight_grad, downweight_grad, projweight_grad, qkvweight_grad)
    )
    projweight_grad, qkvweight_grad = lax.psum((projweight_grad, qkvweight_grad), "rep")
    qkvweight_grad = to_rows(qkvweight_grad, 3)

    return (
        block_out.reshape(images, tok_rows, width),
        tokens_grad.reshape(images, tok_rows, width),
        vectors[0],
        vectors[1],
        qkvweight_grad.astype(jnp.float32),
        biases[:own],
        biases[own : 2 * own],
        projweight_grad.astype(jnp.float32),
        vectors[2],
        vectors[3],
        vectors[4],
        vectors[5],
        upweight_grad.astype(jnp.float32),
        biases[2 * own :],
        downweight_grad.astype(jnp.float32),
        vectors[6],
        vectors[7],
    )


def solution(mesh):
    shards, seqs = mesh.shape["shard"], mesh.shape["seq"]
    if seqs == 2 and HEADS % (shards * seqs) == 0:
        body = functools.partial(tensor_parallel, shards, seqs)
    else:
        body = per_device
    return jax.shard_map(
        body,
        mesh=mesh,
        in_specs=(
            P(("rep", "shard"), "seq", None),
            P(("rep", "shard"), None),
            P(("rep", "shard"), "seq", None),
            P(("shard", "seq")),
            P(("shard", "seq")),
            P(("shard", "seq"), None),
            P(("shard", "seq")),
            P(("shard", "seq")),
            P(("shard", "seq"), None),
            P(("shard", "seq")),
            P(("shard", "seq")),
            P(("shard", "seq")),
            P(("shard", "seq")),
            P(("shard", "seq"), None),
            P(("shard", "seq")),
            P(("shard", "seq"), None),
            P(("shard", "seq")),
            P(("shard", "seq")),
        ),
        out_specs=(
            P(("rep", "shard"), "seq", None),
            P(("rep", "shard"), "seq", None),
            P(("shard", "seq")),
            P(("shard", "seq")),
            P(("shard", "seq"), None),
            P(("shard", "seq")),
            P(("shard", "seq")),
            P(("shard", "seq"), None),
            P(("shard", "seq")),
            P(("shard", "seq")),
            P(("shard", "seq")),
            P(("shard", "seq")),
            P(("shard", "seq"), None),
            P(("shard", "seq")),
            P(("shard", "seq"), None),
            P(("shard", "seq")),
            P(("shard", "seq")),
        ),
        check_vma=False,
    )
```

```python
import functools

import jax
import jax.numpy as jnp
from jax import lax
from jax.experimental import pallas as pl
from jax.experimental.pallas import tpu as pltpu
from jax.sharding import PartitionSpec as P

HEADS = 16
HEAD = 64


EPSILON = 1e-06
SCORE_SCALE = 0.125
ROOT_HALF = 0.7071067811865476
INV_ROOT_TAU = 0.3989422804014327
MASKED = -1e30


def norm_forward(hidden):
    center = hidden - jnp.mean(hidden, axis=-1, keepdims=True)
    spread = lax.rsqrt(jnp.mean(center * center, axis=-1, keepdims=True) + EPSILON)
    return (center * spread, spread)


def norm_backward(grad_norm, normed, spread):
    first_mean = jnp.mean(grad_norm, axis=-1, keepdims=True)
    second_mean = jnp.mean(grad_norm * normed, axis=-1, keepdims=True)
    return spread * (grad_norm - first_mean - normed * second_mean)


def gelu_pair(hidden):
    cumulative = 0.5 * (1.0 + lax.erf(hidden * ROOT_HALF))
    gelu_slope = cumulative + hidden * jnp.exp(-0.5 * hidden * hidden) * INV_ROOT_TAU
    return (hidden * cumulative, gelu_slope)


def split_heads(matrix, images):
    return matrix.reshape(images, -1, HEADS, HEAD)


def score_block(query_heads, key_heads, key_valid):
    scores = (
        jnp.einsum("iqhe,ikhe->ihqk", query_heads, key_heads, preferred_element_type=jnp.float32)
        * SCORE_SCALE
    )
    return jnp.where((key_valid > 0)[:, None, None, :], scores, MASKED)


def contract_rows(left, right):
    return lax.dot_general(
        left, right, (((0,), (0,)), ((), ())), preferred_element_type=jnp.float32
    )


def times_transposed(left, weight):
    return lax.dot_general(
        left, weight, (((1,), (1,)), ((), ())), preferred_element_type=jnp.float32
    )


def per_device(
    tokens,
    key_valid,
    cotangent,
    attngain,
    attnshift,
    qkvweight,
    querybias,
    valuebias,
    projweight,
    projbias,
    attnscale,
    mlpgain,
    mlpshift,
    upweight,
    upbias,
    downweight,
    downbias,
    mlpscale,
):
    images, tok_rows, feat_width = tokens.shape
    total_rows = images * tok_rows
    gain_one, shift_one, qkv_full, qbias_full, vbias_full, proj_full, pbias_full, scale_one = (
        lax.all_gather(attngain, ("shard", "seq"), axis=0, tiled=True),
        lax.all_gather(attnshift, ("shard", "seq"), axis=0, tiled=True),
        lax.all_gather(qkvweight, ("shard", "seq"), axis=0, tiled=True),
        lax.all_gather(querybias, ("shard", "seq"), axis=0, tiled=True),
        lax.all_gather(valuebias, ("shard", "seq"), axis=0, tiled=True),
        lax.all_gather(projweight, ("shard", "seq"), axis=0, tiled=True),
        lax.all_gather(projbias, ("shard", "seq"), axis=0, tiled=True),
        lax.all_gather(attnscale, ("shard", "seq"), axis=0, tiled=True),
    )
    hidden = tokens.reshape(total_rows, feat_width).astype(jnp.float32)
    normed_one, spread_one = norm_forward(hidden)
    act_one = (normed_one * gain_one.astype(jnp.float32) + shift_one.astype(jnp.float32)).astype(
        jnp.bfloat16
    )
    mixed = jnp.dot(act_one, qkv_full, preferred_element_type=jnp.float32)
    queries = (mixed[:, :feat_width] + qbias_full.astype(jnp.float32)).astype(jnp.bfloat16)
    key_local = (
        mixed[:, feat_width : 2 * feat_width]
        .astype(jnp.bfloat16)
        .reshape(images, tok_rows, feat_width)
    )
    value_local = (
        (mixed[:, 2 * feat_width :] + vbias_full.astype(jnp.float32))
        .astype(jnp.bfloat16)
        .reshape(images, tok_rows, feat_width)
    )
    key_all, value_all = (
        lax.all_gather(key_local, "seq", axis=1, tiled=True),
        lax.all_gather(value_local, "seq", axis=1, tiled=True),
    )
    query_heads = split_heads(queries, images)
    key_heads = split_heads(key_all, images)
    value_heads = split_heads(value_all, images)
    scores = score_block(query_heads, key_heads, key_valid)
    top_score = jnp.max(scores, axis=-1, keepdims=True)
    log_total = top_score + jnp.log(jnp.sum(jnp.exp(scores - top_score), axis=-1, keepdims=True))
    prob_low = jnp.exp(scores - log_total).astype(jnp.bfloat16)
    attended = (
        jnp.einsum("ihqk,ikhe->iqhe", prob_low, value_heads, preferred_element_type=jnp.float32)
        .reshape(total_rows, feat_width)
        .astype(jnp.bfloat16)
    )
    branch_one = jnp.dot(
        attended, proj_full, preferred_element_type=jnp.float32
    ) + pbias_full.astype(jnp.float32)
    middle = hidden + scale_one.astype(jnp.float32) * branch_one
    gain_two, shift_two, up_full, upb_full, down_full, downb_full, scale_two = (
        lax.all_gather(mlpgain, ("shard", "seq"), axis=0, tiled=True),
        lax.all_gather(mlpshift, ("shard", "seq"), axis=0, tiled=True),
        lax.all_gather(upweight, ("shard", "seq"), axis=0, tiled=True),
        lax.all_gather(upbias, ("shard", "seq"), axis=0, tiled=True),
        lax.all_gather(downweight, ("shard", "seq"), axis=0, tiled=True),
        lax.all_gather(downbias, ("shard", "seq"), axis=0, tiled=True),
        lax.all_gather(mlpscale, ("shard", "seq"), axis=0, tiled=True),
    )
    normed_two, spread_two = norm_forward(middle)
    act_two = (normed_two * gain_two.astype(jnp.float32) + shift_two.astype(jnp.float32)).astype(
        jnp.bfloat16
    )
    inner_pre = jnp.dot(act_two, up_full, preferred_element_type=jnp.float32) + upb_full.astype(
        jnp.float32
    )
    activated, gelu_slope = gelu_pair(inner_pre)
    act_three = activated.astype(jnp.bfloat16)
    branch_two = jnp.dot(
        act_three, down_full, preferred_element_type=jnp.float32
    ) + downb_full.astype(jnp.float32)
    block_out = middle + scale_two.astype(jnp.float32) * branch_two
    out_grad = cotangent.reshape(total_rows, feat_width).astype(jnp.float32)
    mlpscale_grad = jnp.sum(out_grad * branch_two, axis=0)
    branch_grad = out_grad * scale_two.astype(jnp.float32)
    downbias_grad = jnp.sum(branch_grad, axis=0)
    branch_low = branch_grad.astype(jnp.bfloat16)
    downweight_grad = contract_rows(act_three, branch_low)
    inner_grad = times_transposed(branch_low, down_full) * gelu_slope
    upbias_grad = jnp.sum(inner_grad, axis=0)
    inner_low = inner_grad.astype(jnp.bfloat16)
    upweight_grad = contract_rows(act_two, inner_low)
    acttwo_grad = times_transposed(inner_low, up_full)
    mlpgain_grad = jnp.sum(acttwo_grad * normed_two, axis=0)
    mlpshift_grad = jnp.sum(acttwo_grad, axis=0)
    middle_grad = out_grad + norm_backward(
        acttwo_grad * gain_two.astype(jnp.float32), normed_two, spread_two
    )
    mlp_part = (
        lax.psum_scatter(mlpgain_grad, ("shard", "seq"), scatter_dimension=0, tiled=True),
        lax.psum_scatter(mlpshift_grad, ("shard", "seq"), scatter_dimension=0, tiled=True),
        lax.psum_scatter(upweight_grad, ("shard", "seq"), scatter_dimension=0, tiled=True),
        lax.psum_scatter(upbias_grad, ("shard", "seq"), scatter_dimension=0, tiled=True),
        lax.psum_scatter(downweight_grad, ("shard", "seq"), scatter_dimension=0, tiled=True),
        lax.psum_scatter(downbias_grad, ("shard", "seq"), scatter_dimension=0, tiled=True),
        lax.psum_scatter(mlpscale_grad, ("shard", "seq"), scatter_dimension=0, tiled=True),
    )
    mlp_total = lax.psum(
        (mlp_part[0], mlp_part[1], mlp_part[2], mlp_part[3], mlp_part[4], mlp_part[5], mlp_part[6]),
        "rep",
    )
    attnscale_grad = jnp.sum(middle_grad * branch_one, axis=0)
    branchone_grad = middle_grad * scale_one.astype(jnp.float32)
    projbias_grad = jnp.sum(branchone_grad, axis=0)
    proj_low = branchone_grad.astype(jnp.bfloat16)
    projweight_grad = contract_rows(attended, proj_low)
    attn_back = times_transposed(proj_low, proj_full).astype(jnp.bfloat16)
    back_heads = split_heads(attn_back, images)
    scores = score_block(query_heads, key_heads, key_valid)
    probs = jnp.exp(scores - log_total)
    prob_low = probs.astype(jnp.bfloat16)
    prob_grad = jnp.einsum(
        "iqhe,ikhe->ihqk", back_heads, value_heads, preferred_element_type=jnp.float32
    )
    row_dot = jnp.sum(probs * prob_grad, axis=-1, keepdims=True)
    score_low = (probs * (prob_grad - row_dot)).astype(jnp.bfloat16)
    query_grad = (
        jnp.einsum("ihqk,ikhe->iqhe", score_low, key_heads, preferred_element_type=jnp.float32)
        * SCORE_SCALE
    ).reshape(total_rows, feat_width)
    key_part = (
        jnp.einsum("ihqk,iqhe->ikhe", score_low, query_heads, preferred_element_type=jnp.float32)
        * SCORE_SCALE
    ).reshape(images, -1, feat_width)
    value_part = jnp.einsum(
        "ihqk,iqhe->ikhe", prob_low, back_heads, preferred_element_type=jnp.float32
    ).reshape(images, -1, feat_width)
    key_grad, value_grad = (
        lax.psum_scatter(key_part, "seq", scatter_dimension=1, tiled=True),
        lax.psum_scatter(value_part, "seq", scatter_dimension=1, tiled=True),
    )
    key_grad = key_grad.reshape(total_rows, feat_width)
    value_grad = value_grad.reshape(total_rows, feat_width)
    querybias_grad = jnp.sum(query_grad, axis=0)
    valuebias_grad = jnp.sum(value_grad, axis=0)
    mixed_low = jnp.concatenate([query_grad, key_grad, value_grad], axis=1).astype(jnp.bfloat16)
    qkvweight_grad = contract_rows(act_one, mixed_low)
    actone_grad = times_transposed(mixed_low, qkv_full)
    attngain_grad = jnp.sum(actone_grad * normed_one, axis=0)
    attnshift_grad = jnp.sum(actone_grad, axis=0)
    tokens_grad = middle_grad + norm_backward(
        actone_grad * gain_one.astype(jnp.float32), normed_one, spread_one
    )
    attn_part = (
        lax.psum_scatter(attngain_grad, ("shard", "seq"), scatter_dimension=0, tiled=True),
        lax.psum_scatter(attnshift_grad, ("shard", "seq"), scatter_dimension=0, tiled=True),
        lax.psum_scatter(qkvweight_grad, ("shard", "seq"), scatter_dimension=0, tiled=True),
        lax.psum_scatter(querybias_grad, ("shard", "seq"), scatter_dimension=0, tiled=True),
        lax.psum_scatter(valuebias_grad, ("shard", "seq"), scatter_dimension=0, tiled=True),
        lax.psum_scatter(projweight_grad, ("shard", "seq"), scatter_dimension=0, tiled=True),
        lax.psum_scatter(projbias_grad, ("shard", "seq"), scatter_dimension=0, tiled=True),
        lax.psum_scatter(attnscale_grad, ("shard", "seq"), scatter_dimension=0, tiled=True),
    )
    attn_total = lax.psum(
        (
            attn_part[0],
            attn_part[1],
            attn_part[2],
            attn_part[3],
            attn_part[4],
            attn_part[5],
            attn_part[6],
            attn_part[7],
        ),
        "rep",
    )
    return (
        block_out.reshape(images, tok_rows, feat_width),
        tokens_grad.reshape(images, tok_rows, feat_width),
        attn_total[0],
        attn_total[1],
        attn_total[2],
        attn_total[3],
        attn_total[4],
        attn_total[5],
        attn_total[6],
        attn_total[7],
        mlp_total[0],
        mlp_total[1],
        mlp_total[2],
        mlp_total[3],
        mlp_total[4],
        mlp_total[5],
        mlp_total[6],
    )


GROUP = ("shard", "seq")


def gather_rows(array):
    return lax.all_gather(array, GROUP, axis=0, tiled=True)


VMEM_LIMIT = 40 * 1024 * 1024


def chip_barrier(shards, shard, other):
    barrier = pltpu.get_barrier_semaphore()
    for step in range(1, shards):
        pl.semaphore_signal(
            barrier, inc=1, device_id={"shard": lax.rem(shard + step, shards)}
        )
    pl.semaphore_signal(barrier, inc=1, device_id={"seq": other})
    pl.semaphore_wait(barrier, shards)


def gather_kernel(shards, count, *refs):
    sources, results = refs[:count], refs[count : 2 * count]
    send_sem, recv_sem, local_sem = refs[2 * count :]
    shard, seq = lax.axis_index("shard"), lax.axis_index("seq")
    other = 1 - seq
    place = 2 * shard + seq
    chip_barrier(shards, shard, other)

    def push(source, target, slot, device):
        copy = pltpu.make_async_remote_copy(
            src_ref=source,
            dst_ref=target,
            send_sem=send_sem.at[slot],
            recv_sem=recv_sem.at[slot],
            device_id=device,
        )
        copy.start()
        return copy

    slots = 2 * shards - 1
    along, pending, local = {}, [], []
    for at in range(count):
        for step in range(1, shards):
            along[at, step] = push(
                sources[at],
                results[at].at[place],
                at * slots + step - 1,
                {"shard": lax.rem(shard + step, shards)},
            )
        pending.append(
            push(sources[at], results[at].at[place], at * slots + shards - 1, {"seq": other})
        )
        copy = pltpu.make_async_copy(sources[at], results[at].at[place], local_sem.at[at])
        copy.start()
        local.append(copy)
    for at in range(count):
        for step in range(1, shards):
            along[at, step].wait_recv()
            origin = 2 * lax.rem(shard + shards - step, shards) + seq
            pending.append(
                push(
                    results[at].at[origin],
                    results[at].at[origin],
                    at * slots + shards - 1 + step,
                    {"seq": other},
                )
            )
    for copy in local:
        copy.wait()
    for copy in along.values():
        copy.wait_send()
    for copy in pending:
        copy.wait()


def gather_group(shards, call, *arrays):
    count = len(arrays)
    copies = count * (2 * shards - 1)
    results = pl.pallas_call(
        functools.partial(gather_kernel, shards, count),
        out_shape=[
            jax.ShapeDtypeStruct((2 * shards,) + array.shape, array.dtype) for array in arrays
        ],
        in_specs=[pl.BlockSpec(memory_space=pltpu.VMEM)] * count,
        out_specs=[pl.BlockSpec(memory_space=pltpu.VMEM)] * count,
        scratch_shapes=[
            pltpu.SemaphoreType.DMA((copies,)),
            pltpu.SemaphoreType.DMA((copies,)),
            pltpu.SemaphoreType.DMA((count,)),
        ],
        compiler_params=pltpu.CompilerParams(
            collective_id=call, has_side_effects=True, vmem_limit_bytes=VMEM_LIMIT
        ),
        name="gather_group_%d" % call,
    )(*arrays)
    return results


def scatter_kernel(shards, terms, total, near, outgoing, arrived, send_sem, recv_sem):
    shard, seq = lax.axis_index("shard"), lax.axis_index("seq")
    other = 1 - seq
    chip_barrier(shards, shard, other)

    def push(source, target, slot, device):
        copy = pltpu.make_async_remote_copy(
            src_ref=source,
            dst_ref=target,
            send_sem=send_sem.at[slot],
            recv_sem=recv_sem.at[slot],
            device_id=device,
        )
        copy.start()
        return copy

    first, second = [], []
    for step in range(1, shards + 1):
        target = lax.rem(shard + step, shards)
        first.append(
            push(terms.at[2 * target + other], near.at[step - 1], step - 1, {"seq": other})
        )
    for step in range(1, shards + 1):
        target = lax.rem(shard + step, shards)
        first[step - 1].wait_recv()
        both = terms[2 * target + seq].astype(jnp.float32) + near[step - 1].astype(jnp.float32)
        if step == shards:
            total[...] = both
        else:
            outgoing[step - 1] = both.astype(jnp.bfloat16)
            second.append(
                push(
                    outgoing.at[step - 1],
                    arrived.at[step - 1],
                    shards + step - 1,
                    {"shard": target},
                )
            )
    for step in range(1, shards):
        second[step - 1].wait_recv()
        total[...] += arrived[step - 1].astype(jnp.float32)
    for copy in first + second:
        copy.wait_send()


def scatter_group(shards, call, terms):
    terms = terms.astype(jnp.bfloat16)
    rows, columns = terms.shape
    block = (rows // (2 * shards), columns)
    copies = 2 * shards - 1
    return pl.pallas_call(
        functools.partial(scatter_kernel, shards),
        out_shape=jax.ShapeDtypeStruct(block, jnp.float32),
        in_specs=[pl.BlockSpec(memory_space=pltpu.VMEM)],
        out_specs=pl.BlockSpec(memory_space=pltpu.VMEM),
        scratch_shapes=[
            pltpu.VMEM((shards,) + block, jnp.bfloat16),
            pltpu.VMEM((shards - 1,) + block, jnp.bfloat16),
            pltpu.VMEM((shards - 1,) + block, jnp.bfloat16),
            pltpu.SemaphoreType.DMA((copies,)),
            pltpu.SemaphoreType.DMA((copies,)),
        ],
        compiler_params=pltpu.CompilerParams(
            collective_id=call, has_side_effects=True, vmem_limit_bytes=VMEM_LIMIT
        ),
        name="scatter_group_%d" % call,
    )(terms.reshape((2 * shards,) + block))


def exchange_kernel(shards, reps, with_scatter, *refs):
    if with_scatter:
        main, column, row, vectors, biases = refs[:5]
        result, column_out, row_out, vectors_out = refs[5:9]
        near, outgoing, arrived, column_near, column_sum, row_near, vector_in, vector_sum = refs[
            9:17
        ]
        rest = refs[17:]
        vector_near, rest = rest[0], rest[1:]
    else:
        main, column, row = refs[:3]
        result, column_out, row_out = refs[3:6]
        column_near, column_sum, row_near = refs[6:9]
        rest = refs[9:]
    send_sem, recv_sem, local_sem = rest
    group = 2 * shards
    rep = lax.axis_index("rep")
    shard, seq = lax.axis_index("shard"), lax.axis_index("seq")
    other = 1 - seq
    place = 2 * shard + seq

    def member(step):
        at = lax.rem(place + step, group)
        return at, {"shard": at // 2, "seq": lax.rem(at, 2)}

    barrier = pltpu.get_barrier_semaphore()
    for step in range(1, group):
        pl.semaphore_signal(barrier, inc=1, device_id=member(step)[1])
    for step in range(1, reps):
        pl.semaphore_signal(barrier, inc=1, device_id={"rep": lax.rem(rep + step, reps)})
    pl.semaphore_wait(barrier, group + reps - 2)

    used = []

    def push(source, target, device):
        slot = len(used)
        copy = pltpu.make_async_remote_copy(
            src_ref=source,
            dst_ref=target,
            send_sem=send_sem.at[slot],
            recv_sem=recv_sem.at[slot],
            device_id=device,
        )
        copy.start()
        used.append(copy)
        return copy

    def peer(step):
        return lax.rem(rep + step, reps)

    first, along, local = [], [], []
    if with_scatter:
        for step in range(1, shards + 1):
            target = lax.rem(shard + step, shards)
            first.append(push(main.at[2 * target + other], near.at[step - 1], {"seq": other}))
    else:
        for step in range(1, shards):
            along.append(
                push(main, result.at[place], {"shard": lax.rem(shard + step, shards)})
            )
        beside = push(main, result.at[place], {"seq": other})
        copy = pltpu.make_async_copy(main, result.at[place], local_sem.at[0])
        copy.start()
        local.append(copy)
    column_first = [
        push(column.at[:, peer(step)], column_near.at[step - 1], {"rep": peer(step)})
        for step in range(1, reps)
    ]
    row_first = [
        push(row.at[peer(step)], row_near.at[step - 1], {"rep": peer(step)})
        for step in range(1, reps)
    ]
    if with_scatter:
        vector_first = []
        for step in range(1, group):
            at, device = member(step)
            vector_first.append(push(vectors.at[at], vector_in.at[step - 1], device))

    last = []
    if with_scatter:
        for step in range(1, shards + 1):
            target = lax.rem(shard + step, shards)
            first[step - 1].wait_recv()
            both = main[2 * target + seq].astype(jnp.float32) + near[step - 1].astype(jnp.float32)
            if step == shards:
                result[...] = both
            else:
                outgoing[step - 1] = both.astype(jnp.bfloat16)
                along.append(
                    push(outgoing.at[step - 1], arrived.at[step - 1], {"shard": target})
                )
        half = vectors.shape[1]
        total = vectors[place]
        for step in range(1, group):
            vector_first[step - 1].wait_recv()
            total += vector_in[step - 1]
        vector_sum[:half] = total
        vector_sum[half:] = biases[...]
        vector_second = [
            push(vector_sum, vector_near.at[step - 1], {"rep": peer(step)})
            for step in range(1, reps)
        ]
    else:
        for step in range(1, shards):
            along[step - 1].wait_recv()
            origin = 2 * lax.rem(shard + shards - step, shards) + seq
            last.append(push(result.at[origin], result.at[origin], {"seq": other}))
        last.append(beside)

    for copy in column_first:
        copy.wait_recv()
    total = column[:, rep].astype(jnp.float32)
    for step in range(1, reps):
        total += column_near[step - 1].astype(jnp.float32)
    column_sum[...] = total.astype(jnp.bfloat16)
    column_second = []
    for step in range(1, group):
        at, device = member(step)
        column_second.append(push(column_sum.at[at], column_out.at[place, rep], device))
    copy = pltpu.make_async_copy(column_sum.at[place], column_out.at[place, rep], local_sem.at[1])
    copy.start()

    for row_copy in row_first:
        row_copy.wait_recv()
    total = row[rep].astype(jnp.float32)
    for step in range(1, reps):
        total += row_near[step - 1].astype(jnp.float32)
    row_out[rep] = total.astype(jnp.bfloat16)
    for step in range(1, reps):
        last.append(push(row_out.at[rep], row_out.at[rep], {"rep": peer(step)}))

    copy.wait()
    for column_copy in column_second:
        column_copy.wait_recv()
    for step in range(1, reps):
        last.append(
            push(column_out.at[:, rep], column_out.at[:, rep], {"rep": peer(step)})
        )
    if with_scatter:
        for step in range(1, reps):
            vector_second[step - 1].wait_recv()
        total = vector_sum[...]
        for step in range(1, reps):
            total += vector_near[step - 1]
        vectors_out[...] = total
        for step in range(1, shards):
            along[step - 1].wait_recv()
            result[...] += arrived[step - 1].astype(jnp.float32)
    for local_copy in local:
        local_copy.wait()
    for done in last:
        done.wait_recv()
    for done in used:
        done.wait_send()


def exchange(shards, reps, call, main, column, row, vectors=None, biases=None):
    with_scatter = vectors is not None
    group = 2 * shards
    column = column.reshape(group, reps, column.shape[0] // (group * reps), -1)
    row = row.reshape(reps, row.shape[0] // reps, -1)
    part = (group,) + column.shape[2:]
    low = jnp.bfloat16
    scratch = [
        pltpu.VMEM((reps - 1,) + part, low),
        pltpu.VMEM(part, low),
        pltpu.VMEM((reps - 1,) + row.shape[1:], low),
    ]
    outs = [jax.ShapeDtypeStruct(column.shape, low), jax.ShapeDtypeStruct(row.shape, low)]
    operands = [column, row]
    copies = 2 * (reps - 1) + (group - 1) + 2 * (reps - 1)
    if with_scatter:
        block = (main.shape[0] // group, main.shape[1])
        main = main.astype(low).reshape((group,) + block)
        summed = (vectors.shape[1] + biases.shape[0], vectors.shape[2])
        scratch = [
            pltpu.VMEM((shards,) + block, low),
            pltpu.VMEM((shards - 1,) + block, low),
            pltpu.VMEM((shards - 1,) + block, low),
        ] + scratch
        scratch += [
            pltpu.VMEM((group - 1,) + vectors.shape[1:], jnp.float32),
            pltpu.VMEM(summed, jnp.float32),
            pltpu.VMEM((reps - 1,) + summed, jnp.float32),
        ]
        operands += [vectors, biases]
        outs = [jax.ShapeDtypeStruct(block, jnp.float32)] + outs
        outs += [jax.ShapeDtypeStruct(summed, jnp.float32)]
        copies += (2 * shards - 1) + (group - 1) + (reps - 1)
    else:
        outs = [jax.ShapeDtypeStruct((group,) + main.shape, main.dtype)] + outs
        copies += 2 * shards - 1
    operands = [main] + operands
    return pl.pallas_call(
        functools.partial(exchange_kernel, shards, reps, with_scatter),
        out_shape=outs,
        in_specs=[pl.BlockSpec(memory_space=pltpu.VMEM)] * len(operands),
        out_specs=[pl.BlockSpec(memory_space=pltpu.VMEM)] * len(outs),
        scratch_shapes=scratch
        + [
            pltpu.SemaphoreType.DMA((copies,)),
            pltpu.SemaphoreType.DMA((copies,)),
            pltpu.SemaphoreType.DMA((2,)),
        ],
        compiler_params=pltpu.CompilerParams(
            collective_id=call, has_side_effects=True, vmem_limit_bytes=VMEM_LIMIT
        ),
        name="exchange_%d" % call,
    )(*operands)


def tensor_parallel(reps, shards, seqs, *arguments):
    (
        tokens,
        key_valid,
        cotangent,
        attngain,
        attnshift,
        qkvweight,
        querybias,
        valuebias,
        projweight,
        projbias,
        attnscale,
        mlpgain,
        mlpshift,
        upweight,
        upbias,
        downweight,
        downbias,
        mlpscale,
    ) = arguments
    group = shards * seqs
    images, tok_rows, width = tokens.shape
    rows = images * tok_rows
    own = width // group
    length = key_valid.shape[1]
    group_images = shards * images
    own_heads = HEADS // group

    small = jnp.concatenate(
        [
            attngain,
            attnshift,
            projbias,
            attnscale,
            mlpgain,
            mlpshift,
            downbias,
            mlpscale,
            key_valid.reshape(-1).astype(jnp.bfloat16),
        ]
    )
    used = small.shape[0]
    padded = -(-used // 2048) * 2048
    small = jnp.pad(small, (0, padded - used)).reshape(-1, 128)
    tokens_local = tokens.reshape(rows, width)
    tokens_all, small_all = gather_group(shards, 0, tokens_local, small)
    tokens_all = tokens_all.reshape(group * rows, width)
    small_all = small_all.reshape(group, padded)

    def vector(at):
        return small_all[:, at * own : (at + 1) * own].reshape(width).astype(jnp.float32)

    gain_one, shift_one, bias_proj, scale_one, gain_two, shift_two, bias_down, scale_two = [
        vector(at) for at in range(8)
    ]
    valid = small_all[:, 8 * own : used].reshape(shards, seqs, images, length)[:, 0]
    valid = valid.reshape(group_images, length)

    def to_images(matrix):
        matrix = matrix.reshape(shards, seqs, images, tok_rows, own_heads, HEAD)
        return matrix.transpose(0, 2, 1, 3, 4, 5).reshape(group_images, length, own_heads, HEAD)

    def from_images(heads):
        heads = heads.reshape(shards, images, seqs, tok_rows, own)
        return heads.transpose(0, 2, 1, 3, 4).reshape(group * rows, own)

    def to_columns(weight, parts):
        split = weight.reshape(own, parts, group, -1)
        moved = lax.all_to_all(split, GROUP, split_axis=2, concat_axis=0, tiled=True)
        return moved.reshape(width, -1)

    def to_rows(moved, parts):
        moved = moved.reshape(group, own, parts, -1).transpose(1, 2, 0, 3)
        return moved.reshape(own, -1).astype(jnp.float32)

    qkv_own = to_columns(qkvweight, 3)
    up_own = to_columns(upweight, 1)
    cot_all = gather_rows(cotangent.reshape(rows, width))

    normed_one_all, _ = norm_forward(tokens_all.astype(jnp.float32))
    act_one = (normed_one_all * gain_one + shift_one).astype(jnp.bfloat16)
    mixed = jnp.dot(act_one, qkv_own, preferred_element_type=jnp.float32)
    query_heads = to_images((mixed[:, :own] + querybias.astype(jnp.float32)).astype(jnp.bfloat16))
    key_heads = to_images(mixed[:, own : 2 * own].astype(jnp.bfloat16))
    value_heads = to_images(
        (mixed[:, 2 * own :] + valuebias.astype(jnp.float32)).astype(jnp.bfloat16)
    )
    scores = score_block(query_heads, key_heads, valid)
    top_score = jnp.max(scores, axis=-1, keepdims=True)
    log_total = top_score + jnp.log(jnp.sum(jnp.exp(scores - top_score), axis=-1, keepdims=True))
    probs = jnp.exp(scores - log_total)
    prob_low = probs.astype(jnp.bfloat16)
    attended = from_images(
        jnp.einsum(
            "ihqk,ikhe->iqhe", prob_low, value_heads, preferred_element_type=jnp.float32
        ).astype(jnp.bfloat16)
    )
    branch_one = (
        scatter_group(shards, 1, jnp.dot(attended, projweight, preferred_element_type=jnp.float32)) + bias_proj
    )
    hidden = tokens_local.astype(jnp.float32)
    normed_one, spread_one = norm_forward(hidden)
    middle = hidden + scale_one * branch_one
    normed_two, spread_two = norm_forward(middle)
    act_two = gather_group(
        shards, 2, (normed_two * gain_two + shift_two).astype(jnp.bfloat16)
    )[0].reshape(group * rows, width)

    inner_pre = jnp.dot(act_two, up_own, preferred_element_type=jnp.float32) + upbias.astype(
        jnp.float32
    )
    activated, gelu_slope = gelu_pair(inner_pre)
    act_three = activated.astype(jnp.bfloat16)
    branch_low = (cot_all.astype(jnp.float32) * scale_two).astype(jnp.bfloat16)
    inner_grad = times_transposed(branch_low, downweight) * gelu_slope
    inner_low = inner_grad.astype(jnp.bfloat16)
    acttwo_grad = scatter_group(shards, 3, times_transposed(inner_low, up_own))
    branch_two = (
        scatter_group(shards, 4, jnp.dot(act_three, downweight, preferred_element_type=jnp.float32)) + bias_down
    )
    upbias_grad = jnp.sum(inner_grad, axis=0)
    downweight_grad = contract_rows(act_three, branch_low).astype(jnp.bfloat16)
    upweight_grad = contract_rows(act_two, inner_low).astype(jnp.bfloat16)
    out_grad = cotangent.reshape(rows, width).astype(jnp.float32)
    middle_grad = out_grad + norm_backward(acttwo_grad * gain_two, normed_two, spread_two)
    branchone_grad = middle_grad * scale_one
    proj_low, upweight_grad, downweight_grad = exchange(
        shards,
        reps,
        5,
        branchone_grad.astype(jnp.bfloat16),
        upweight_grad,
        downweight_grad,
    )
    proj_low = proj_low.reshape(group * rows, width)
    upweight_grad = to_rows(upweight_grad, 1)
    downweight_grad = downweight_grad.reshape(-1, width).astype(jnp.float32)

    block_out = middle + scale_two * branch_two

    back_heads = to_images(times_transposed(proj_low, projweight).astype(jnp.bfloat16))
    projweight_grad = contract_rows(attended, proj_low).astype(jnp.bfloat16)
    prob_grad = jnp.einsum(
        "iqhe,ikhe->ihqk", back_heads, value_heads, preferred_element_type=jnp.float32
    )
    row_dot = jnp.sum(probs * prob_grad, axis=-1, keepdims=True)
    score_low = (probs * (prob_grad - row_dot)).astype(jnp.bfloat16)
    query_grad = from_images(
        jnp.einsum("ihqk,ikhe->iqhe", score_low, key_heads, preferred_element_type=jnp.float32)
        * SCORE_SCALE
    )
    key_grad = from_images(
        jnp.einsum("ihqk,iqhe->ikhe", score_low, query_heads, preferred_element_type=jnp.float32)
        * SCORE_SCALE
    )
    value_grad = from_images(
        jnp.einsum("ihqk,iqhe->ikhe", prob_low, back_heads, preferred_element_type=jnp.float32)
    )
    mixed_low = jnp.concatenate([query_grad, key_grad, value_grad], axis=1).astype(jnp.bfloat16)
    actone_part = times_transposed(mixed_low, qkv_own)
    qkvweight_grad = contract_rows(act_one, mixed_low).astype(jnp.bfloat16)
    vectors = jnp.stack(
        [
            jnp.sum(actone_part * normed_one_all, axis=0),
            jnp.sum(actone_part, axis=0),
            jnp.sum(branchone_grad, axis=0),
            jnp.sum(middle_grad * branch_one, axis=0),
            jnp.sum(acttwo_grad * normed_two, axis=0),
            jnp.sum(acttwo_grad, axis=0),
            jnp.sum(out_grad * scale_two, axis=0),
            jnp.sum(out_grad * branch_two, axis=0),
        ]
    )
    biases = jnp.concatenate(
        [jnp.sum(query_grad, axis=0), jnp.sum(value_grad, axis=0), upbias_grad]
    )
    used = biases.shape[0]
    padded = -(-used // (8 * own)) * 8 * own
    biases = jnp.pad(biases, (0, padded - used)).reshape(-1, own)
    actone_grad, qkvweight_grad, projweight_grad, totals = exchange(
        shards,
        reps,
        6,
        actone_part,
        qkvweight_grad,
        projweight_grad,
        vectors.reshape(8, group, own).transpose(1, 0, 2),
        biases,
    )
    tokens_grad = middle_grad + norm_backward(actone_grad * gain_one, normed_one, spread_one)
    vectors = totals[:8]
    biases = totals[8:].reshape(-1)[:used]
    qkvweight_grad = to_rows(qkvweight_grad, 3)
    projweight_grad = projweight_grad.reshape(own, width).astype(jnp.float32)

    return (
        block_out.reshape(images, tok_rows, width),
        tokens_grad.reshape(images, tok_rows, width),
        vectors[0],
        vectors[1],
        qkvweight_grad,
        biases[:own],
        biases[own : 2 * own],
        projweight_grad,
        vectors[2],
        vectors[3],
        vectors[4],
        vectors[5],
        upweight_grad,
        biases[2 * own :],
        downweight_grad,
        vectors[6],
        vectors[7],
    )


def solution(mesh):
    shards, seqs = mesh.shape["shard"], mesh.shape["seq"]
    if seqs == 2 and HEADS % (shards * seqs) == 0:
        body = functools.partial(tensor_parallel, mesh.shape["rep"], shards, seqs)
    else:
        body = per_device
    return jax.shard_map(
        body,
        mesh=mesh,
        in_specs=(
            P(("rep", "shard"), "seq", None),
            P(("rep", "shard"), None),
            P(("rep", "shard"), "seq", None),
            P(("shard", "seq")),
            P(("shard", "seq")),
            P(("shard", "seq"), None),
            P(("shard", "seq")),
            P(("shard", "seq")),
            P(("shard", "seq"), None),
            P(("shard", "seq")),
            P(("shard", "seq")),
            P(("shard", "seq")),
            P(("shard", "seq")),
            P(("shard", "seq"), None),
            P(("shard", "seq")),
            P(("shard", "seq"), None),
            P(("shard", "seq")),
            P(("shard", "seq")),
        ),
        out_specs=(
            P(("rep", "shard"), "seq", None),
            P(("rep", "shard"), "seq", None),
            P(("shard", "seq")),
            P(("shard", "seq")),
            P(("shard", "seq"), None),
            P(("shard", "seq")),
            P(("shard", "seq")),
            P(("shard", "seq"), None),
            P(("shard", "seq")),
            P(("shard", "seq")),
            P(("shard", "seq")),
            P(("shard", "seq")),
            P(("shard", "seq"), None),
            P(("shard", "seq")),
            P(("shard", "seq"), None),
            P(("shard", "seq")),
            P(("shard", "seq")),
        ),
        check_vma=False,
    )
```
